128 devices in a mesh: tile: 64 (over z, x, y), view: 2 (over core).
Axes of the slice: x: 4, y: 4, z: 4, core: 2. Of those that a mesh axis runs over, the one named last changes fastest.
Arguments:
- estimate: float32 [1024, 128, 128], P('tile'), may hold values from 0.5 to 2
- view_data: float32 [6, 1024, 128, 128], P('view', 'tile'), may hold values from 0.2 to 5
- psf_taps: float32 [6, 3, 31], P('view'), may hold values from 0.05 to 1
- coverage: int32 [6, 1024], P('view', 'tile'), may hold values 0 or 1
Outputs:
- deconvolved: float32 [1024, 128, 128], P('tile')
The draws below stay inside these ranges and needn't reach their ends.
All inputs are finite; a program needn't handle non-finite values. No bound on the sum of `coverage` on one device may be relied on, other than what follows from the above.
Results may differ from the reference program's by a relative error of at most 0.00012.
Values sent between devices are 32-bit elements; how exact they have to be, the bound alone decides.
No kernel may reach another device: no remote copies, remote signals or barrier semaphores. Data moves between devices by JAX's collectives and lax.ppermute only.
A program may use at most 128 MiB of HBM per device.

```python
import math
import jax
import jax.numpy as jnp
from jax import lax

NY = 128
NZ = 128
TAPS = 31
VIEWS = 6
ITERS = 4
NX = 1024


def set_ends(drawn, stream_key, smallest, top_value):
    dims = drawn.shape
    place = [jax.random.randint(jax.random.fold_in(stream_key, axis), (), 0, dims[axis]) for axis in range(len(dims))]
    drawn = drawn.at[tuple(place)].set(smallest)
    longest = dims.index(max(dims))
    place[longest] = (place[longest] + 1) % dims[longest]
    return drawn.at[tuple(place)].set(top_value)


def block_scale(own_key, dims, split, smallest, high):
    level = 1.0
    for dim, parts in split:
        draws = jax.random.uniform(jax.random.fold_in(jax.random.fold_in(own_key, 6), dim), (parts,), jnp.float32, smallest / len(split), high / len(split))
        level = level * jnp.repeat(jnp.exp(draws), dims[dim] // parts).reshape((-1,) + (1,) * (len(dims) - 1 - dim))
    return level


def setup_inputs(seed: int = 0) -> dict:
    key_list = jax.random.split(jax.random.key(seed), 5)
    return {
        "estimate": jnp.clip(jnp.exp(math.log(2.0) - 1.3862944 * jax.random.uniform(key_list[0], (NX, NY, NZ), jnp.float32) ** block_scale(key_list[0], (NX, NY, NZ), ((0, 64),), -0.2, 0.2)), 0.5, 2.0),
        "view_data": jnp.clip(jnp.exp(math.log(5.0) - 3.218876 * jax.random.uniform(key_list[1], (VIEWS, NX, NY, NZ), jnp.float32) ** block_scale(key_list[1], (VIEWS, NX, NY, NZ), ((0, 2), (1, 64)), -0.2, 0.2)), 0.2, 5.0),
        "psf_taps": jnp.clip(jnp.exp(math.log(1.0) - 2.9957323 * jax.random.uniform(key_list[2], (VIEWS, 3, TAPS), jnp.float32) ** block_scale(key_list[2], (VIEWS, 3, TAPS), ((0, 2),), -0.2, 0.2)), 0.05, 1.0),
        "coverage": set_ends((jax.random.randint(key_list[3], (VIEWS, NX), 0, 2) < 1).astype(jnp.int32), jax.random.fold_in(key_list[3], 1), 0, 1),
    }


def make_band(taps, rows, columns, offset):
    row_index = jnp.arange(rows)[:, None]
    column_index = jnp.arange(columns)[None, :]
    spacing = column_index - row_index + offset
    matrix = jnp.zeros((rows, columns), jnp.float32)
    for lag in range(taps.shape[0]):
        matrix = matrix + taps[lag] * (spacing == lag).astype(jnp.float32)
    return matrix


def forward_blur(volume, x_matrix, y_matrix, z_matrix):
    hp = lax.Precision.HIGHEST
    volume = jnp.einsum('xyz,wx->wyz', volume, x_matrix, precision=hp)
    volume = jnp.einsum('xyz,wy->xwz', volume, y_matrix, precision=hp)
    return jnp.einsum('xyz,wz->xyw', volume, z_matrix, precision=hp)


def adjoint_blur(volume, x_matrix, y_matrix, z_matrix):
    hp = lax.Precision.HIGHEST
    volume = jnp.einsum('xyz,zw->xyw', volume, z_matrix, precision=hp)
    volume = jnp.einsum('xyz,yw->xwz', volume, y_matrix, precision=hp)
    return jnp.einsum('xyz,xw->wyz', volume, x_matrix, precision=hp)


def reference(estimate, view_data, psf_taps, coverage):
    norm_taps = psf_taps / jnp.sum(psf_taps, axis=-1, keepdims=True)
    reach = norm_taps.shape[-1] // 2
    weights = coverage.astype(jnp.float32)
    count = jnp.sum(weights, axis=0)
    keep = 1.0 - jnp.minimum(count, 1.0)
    denom = jnp.maximum(count, 1.0)
    sizes_xyz = estimate.shape
    matrices = []
    for which in range(VIEWS):
        matrices.append([make_band(norm_taps[which, axis_id], sizes_xyz[axis_id], sizes_xyz[axis_id], reach) for axis_id in range(3)])
    current = estimate
    for iteration in range(ITERS):
        total = jnp.zeros_like(current)
        for which in range(VIEWS):
            mats = matrices[which]
            blurred = forward_blur(current, mats[0], mats[1], mats[2])
            ratio = view_data[which] / blurred
            correction = adjoint_blur(ratio, mats[0], mats[1], mats[2])
            total = total + weights[which][:, None, None] * correction
        current = current * (total + keep[:, None, None]) / denom[:, None, None]
    return current
```

```python
import jax
import jax.numpy as jnp
from jax import lax
from jax.experimental import pallas as pl
from jax.experimental.pallas import tpu as pltpu
from jax.sharding import PartitionSpec as P

ITERS = 4
TAPS = 31
REACH = 15
VIEWS = 6
W = 16
HALF = 64
EXT = 96
MID = 80
SLOTS = 48
NZ = 128
F32 = jnp.float32
BF16 = jnp.bfloat16
VMEM = pl.BlockSpec(memory_space=pltpu.VMEM)
SMEM = pl.BlockSpec(memory_space=pltpu.SMEM)


def split(x):
    high = x.astype(BF16)
    return high, (x - high.astype(F32)).astype(BF16)


def dot(a, b):
    return jnp.dot(a, b, preferred_element_type=F32)


def iota(shape, dim):
    return lax.broadcasted_iota(jnp.int32, shape, dim)


def plane_of(slot, core):
    middle = slot - REACH
    swapped = jnp.where(slot < REACH, slot + W, jnp.where(slot < REACH + W, middle, slot - 46))
    return jnp.where(core == 0, middle, swapped)


def row_of(j, core):
    first = jnp.where(j < 32, j + 32, jnp.where(j < 64, j - 32, j))
    second = jnp.where(j < 64, j + 64, j - 32)
    return jnp.where(core == 0, first, second)


def mid_row_of(j, core):
    return jnp.where((core == 1) & (j >= 64), j - 16, row_of(j, core))


def matrices_kernel(where, taps, cover, xf, xt, yf, yt, zf, zt):
    core, tile = where[0], where[1]

    def put(ref, lead, rows, value):
        high, low = split(value)
        ref[lead + (pl.ds(0, rows),)] = high
        ref[lead + (pl.ds(rows, rows),)] = low

    def select(view, axis, index):
        total = jnp.zeros(index.shape, F32)
        for k in range(TAPS):
            total = jnp.where(index == k, taps[(view * 3 + axis) * TAPS + k], total)
        return total

    shape = (VIEWS * W, 2 * SLOTS)
    slot = iota(shape, 1)
    slot = jnp.where(slot < SLOTS, slot, slot - SLOTS)
    plane = plane_of(slot, core)
    at = plane + W * tile
    fine = (slot < 46) & (at >= 0) & (at < 1024)
    row = iota(shape, 0)
    index = jnp.where(fine, plane - row % W + REACH, -1)
    total = jnp.zeros(shape, F32)
    for view in range(VIEWS):
        total = jnp.where(row // W == view, select(view, 0, index), total)
    put(xf, (), VIEWS * W, total)

    shape = (SLOTS, 2 * VIEWS * W)
    slot = iota(shape, 0)
    plane = plane_of(slot, 1 - core)
    at = plane + W * tile
    fine = (slot < 46) & (at >= 0) & (at < 1024)
    column = iota(shape, 1)
    column = jnp.where(column < VIEWS * W, column, column - VIEWS * W)
    index = jnp.where(fine, plane - column % W + REACH, -1)
    total = jnp.zeros(shape, F32)
    for view in range(VIEWS):
        covered = jnp.zeros((SLOTS, 2 * VIEWS * W), F32)
        for p in range(3 * W):
            covered = jnp.where(plane == p - W, cover[(p // W) * VIEWS * W + view * W + p % W], covered)
        total = jnp.where(column // W == view, select(view, 0, index) * covered, total)
    put(xt, (), SLOTS, total)

    def per_view(view, _):
        shape = (MID, 2 * EXT)
        j = iota(shape, 1)
        j = jnp.where(j < EXT, j, j - EXT)
        index = row_of(j, core) - mid_row_of(iota(shape, 0), core) + REACH
        put(yf, (view,), MID, select(view, 1, index))
        shape = (HALF, 2 * MID)
        j = iota(shape, 1)
        j = jnp.where(j < MID, j, j - MID)
        index = row_of(iota(shape, 0), core) - mid_row_of(j, core) + REACH
        put(yt, (view,), HALF, select(view, 1, index))
        difference = iota((NZ, NZ), 0) - iota((NZ, NZ), 1)
        for ref, sign in ((zf, 1), (zt, -1)):
            high, low = split(select(view, 2, sign * difference + REACH))
            for start in (0, NZ):
                ref[view, pl.ds(start, NZ), pl.ds(0, NZ)] = high
                ref[view, pl.ds(start, NZ), pl.ds(NZ, NZ)] = low
        return 0

    lax.fori_loop(0, VIEWS, per_view, 0)


def make_matrices(where, taps, cover):
    shapes = [
        (2 * VIEWS * W, 2 * SLOTS),
        (2 * SLOTS, 2 * VIEWS * W),
        (VIEWS, 2 * MID, 2 * EXT),
        (VIEWS, 2 * HALF, 2 * MID),
        (VIEWS, 2 * NZ, 2 * NZ),
        (VIEWS, 2 * NZ, 2 * NZ),
    ]
    return pl.pallas_call(
        matrices_kernel,
        out_shape=[jax.ShapeDtypeStruct(s, BF16) for s in shapes],
        in_specs=[SMEM, SMEM, SMEM],
        out_specs=[VMEM] * 6,
        compiler_params=pltpu.CompilerParams(vmem_limit_bytes=24 << 20),
        cost_estimate=pl.CostEstimate(flops=4_000_000, bytes_accessed=6_000_000, transcendentals=0),
        name="matrices",
    )(where, taps, cover)


def both(result):
    half = result.shape[0] // 2
    return result[:half] + result[half:]


def correct_kernel(first, own, second, other, data, xf, xt, yf, yt, zf, zt, out1, out_own, out2, ext, mid, wide):
    def place(source, slot, count):
        for i in range(count):
            ext[pl.ds((slot + i) * EXT, HALF)] = source[i]

    place(first, 0, 15)
    place(own, 15, 16)
    place(second, 31, 15)
    for i in range(46):
        ext[pl.ds(i * EXT + HALF, 32)] = other[i]
    for i in range(46, SLOTS):
        ext[pl.ds(i * EXT, EXT)] = jnp.zeros((EXT, NZ), F32)

    group = 4

    def forward_x(step, _):
        parts = [split(ext[pl.ds(step * group + i, SLOTS, stride=EXT)]) for i in range(group)]
        operand = jnp.concatenate(
            [jnp.concatenate([p[0] for p in parts], 1), jnp.concatenate([p[1] for p in parts], 1)], 0
        )
        result = both(dot(xf[...], operand))
        for i in range(group):
            mid[pl.ds(step * group + i, VIEWS * W, stride=EXT)] = result[:, i * NZ : (i + 1) * NZ]
        return 0

    lax.fori_loop(0, EXT // group, forward_x, 0)

    planes = 4

    def inner(step, _):
        view = step // (W // planes)
        start = pl.multiple_of(step * planes * EXT, 8)
        block = mid[pl.ds(start, planes * EXT)]
        result = dot(jnp.concatenate(split(block), 1), zf[view])
        block = result[:, :NZ] + result[:, NZ:]
        high, low = split(block)
        operand = jnp.concatenate(
            [jnp.concatenate([x[i * EXT : (i + 1) * EXT] for i in range(planes)], 1) for x in (high, low)], 0
        )
        blurred = both(dot(yf[view], operand))
        measured = jnp.concatenate([data[step * planes + i] for i in range(planes)], 1)
        high, low = split(measured / blurred)
        result = both(dot(yt[view], jnp.concatenate([high, low], 0)))
        block = jnp.concatenate([result[:, i * NZ : (i + 1) * NZ] for i in range(planes)], 0)
        result = dot(jnp.concatenate(split(block), 1), zt[view])
        block = result[:, :NZ] + result[:, NZ:]
        for i in range(planes):
            mid[pl.ds(start + i * EXT, HALF)] = block[i * HALF : (i + 1) * HALF]
        return 0

    lax.fori_loop(0, VIEWS * W // planes, inner, 0)

    def adjoint_x(step, _):
        parts = [split(mid[pl.ds(step * group + i, VIEWS * W, stride=EXT)]) for i in range(group)]
        operand = jnp.concatenate(
            [jnp.concatenate([p[0] for p in parts], 1), jnp.concatenate([p[1] for p in parts], 1)], 0
        )
        result = both(dot(xt[...], operand))
        for i in range(group):
            wide[pl.ds(step * group + i, SLOTS, stride=HALF)] = result[:, i * NZ : (i + 1) * NZ]
        return 0

    lax.fori_loop(0, HALF // group, adjoint_x, 0)

    for i in range(15):
        out1[i] = wide[pl.ds(i * HALF, HALF)]
        out2[i] = wide[pl.ds((i + 31) * HALF, HALF)]
    for i in range(16):
        out_own[i] = wide[pl.ds((i + 15) * HALF, HALF)]


def correct(first, own, second, other, data, matrices):
    shapes = [(15, HALF, NZ), (16, HALF, NZ), (15, HALF, NZ)]
    return pl.pallas_call(
        correct_kernel,
        out_shape=[jax.ShapeDtypeStruct(s, F32) for s in shapes],
        in_specs=[VMEM] * 11,
        out_specs=[VMEM] * 3,
        scratch_shapes=[
            pltpu.VMEM((SLOTS * EXT, NZ), F32),
            pltpu.VMEM((VIEWS * W * EXT, NZ), F32),
            pltpu.VMEM((SLOTS * HALF, NZ), F32),
        ],
        compiler_params=pltpu.CompilerParams(vmem_limit_bytes=40 << 20),
        cost_estimate=pl.CostEstimate(flops=5_000_000_000, bytes_accessed=16_000_000, transcendentals=0),
        name="correct",
    )(first, own, second, other, data, *matrices)


def update_kernel(where, keep, scale, current, total, from1, from2, new, send1, send2, work):
    core = where[0]
    work[...] = total[...]
    work[pl.ds(core, 15)] += from1[...]
    work[pl.ds(1 - core, 15)] += from2[...]
    for i in range(W):
        new[i] = current[i] * (work[i] + keep[i]) * scale[i]
    send1[...] = new[pl.ds(1 - core, 15)]
    send2[...] = new[pl.ds(core, 15)]


def update(where, keep, scale, current, total, from1, from2):
    shapes = [(16, HALF, NZ), (15, HALF, NZ), (15, HALF, NZ)]
    return pl.pallas_call(
        update_kernel,
        out_shape=[jax.ShapeDtypeStruct(s, F32) for s in shapes],
        in_specs=[SMEM] * 3 + [VMEM] * 4,
        out_specs=[VMEM] * 3,
        scratch_shapes=[pltpu.VMEM((16, HALF, NZ), F32)],
        compiler_params=pltpu.CompilerParams(vmem_limit_bytes=16 << 20),
        cost_estimate=pl.CostEstimate(flops=1_000_000, bytes_accessed=4_000_000, transcendentals=0),
        name="update",
    )(where, keep, scale, current, total, from1, from2)


def neighbours(x, up_core, tiles):
    pairs = []
    for t in range(tiles):
        pairs.append((2 * t + up_core, 2 * ((t + 1) % tiles) + up_core))
        pairs.append((2 * t + 1 - up_core, 2 * ((t - 1) % tiles) + 1 - up_core))
    return lax.ppermute(x, ("tile", "view"), pairs)


def swap(x):
    return lax.ppermute(x, "view", [(0, 1), (1, 0)])


def per_device(estimate, view_data, psf_taps, coverage):
    tiles = lax.axis_size("tile")
    core = lax.axis_index("view")
    tile = lax.axis_index("tile")
    zero = core == 0
    where = jnp.stack([core, tile]).astype(jnp.int32)

    near_rows = jnp.where(zero, estimate[:, 32:64], estimate[:, 64:96])
    far_rows = jnp.where(zero, estimate[:, 0:32], estimate[:, 96:128])
    current = jnp.concatenate([near_rows, far_rows], 1)
    send1 = jnp.where(zero, current[1:], current[:-1])
    send2 = jnp.where(zero, current[:-1], current[1:])

    def rows(who, near):
        low = jnp.where(who, view_data[:, :, 32:64], view_data[:, :, 64:96])
        high = jnp.where(who, view_data[:, :, 0:32], view_data[:, :, 96:128])
        other = jnp.where(who, view_data[:, :, 64:80], view_data[:, :, 48:64])
        return jnp.concatenate([low, high, other], 2)

    data = jnp.concatenate([rows(zero, True), swap(rows(~zero, True))], 0).reshape(VIEWS * W, MID, NZ)

    norm_taps = psf_taps / jnp.sum(psf_taps, axis=-1, keepdims=True)
    weights = coverage.astype(F32)
    mine = jnp.concatenate([norm_taps.reshape(-1), weights.reshape(-1)])
    theirs = swap(mine)
    count = norm_taps.size
    taps = jnp.concatenate([mine[:count], theirs[:count]])
    cover = jnp.concatenate([mine[count:], theirs[count:]])
    ring = [(i, (i + 1) % tiles) for i in range(tiles)]
    back = [(j, i) for i, j in ring]
    swapped = cover.reshape(2, -1)
    before = lax.ppermute(cover, "tile", ring)
    after = lax.ppermute(cover, "tile", back)
    seen = jnp.sum(cover.reshape(VIEWS, W), axis=0)
    keep = 1.0 - jnp.minimum(seen, 1.0)
    scale = 1.0 / jnp.maximum(seen, 1.0)
    matrices = make_matrices(where, taps, jnp.concatenate([before, cover, after]))

    for iteration in range(ITERS):
        first = neighbours(send1, 0, tiles)
        second = neighbours(send2, 1, tiles)
        other = swap(jnp.concatenate([second[:, :32], current[:, :32], first[:, :32]], 0))
        spread1, total, spread2 = correct(first, current, second, other, data, matrices)
        from1 = neighbours(spread1, 0, tiles)
        from2 = neighbours(spread2, 1, tiles)
        current, send1, send2 = update(where, keep, scale, current, total, from1, from2)

    theirs = swap(current)
    low = jnp.where(zero, current, theirs)
    high = jnp.where(zero, theirs, current)
    return jnp.concatenate([low[:, 32:], low[:, :32], high[:, :32], high[:, 32:]], 1)


def solution(mesh):
    return jax.shard_map(
        per_device,
        mesh=mesh,
        in_specs=(
            P("tile", None, None),
            P("view", "tile", None, None),
            P("view", None, None),
            P("view", "tile"),
        ),
        out_specs=P("tile", None, None),
        check_vma=False,
    )
```

```python
import jax
import jax.numpy as jnp
from jax import lax
from jax.experimental import pallas as pl
from jax.experimental.pallas import tpu as pltpu
from jax.sharding import PartitionSpec as P

ITERS = 4
TAPS = 31
REACH = 15
VIEWS = 6
W = 16
HALF = 64
EXT = 96
MID = 80
SLOTS = 48
NZ = 128
OWN_STEP = 65
OTHER_STEP = 33
F32 = jnp.float32
BF16 = jnp.bfloat16
VMEM = pl.BlockSpec(memory_space=pltpu.VMEM)
SMEM = pl.BlockSpec(memory_space=pltpu.SMEM)


def split(x):
    high = x.astype(BF16)
    return high, (x - high.astype(F32)).astype(BF16)


def dot(a, b):
    return jnp.dot(a, b, preferred_element_type=F32)


def iota(shape, dim):
    return lax.broadcasted_iota(jnp.int32, shape, dim)


def plane_of(slot, core):
    middle = slot - REACH
    swapped = jnp.where(slot < REACH, slot + W, jnp.where(slot < REACH + W, middle, slot - 46))
    return jnp.where(core == 0, middle, swapped)


def row_of(j, core):
    first = jnp.where(j < 32, j + 32, jnp.where(j < 64, j - 32, j))
    second = jnp.where(j < 64, j + 64, j - 32)
    return jnp.where(core == 0, first, second)


def mid_row_of(j, core):
    return jnp.where((core == 1) & (j >= 64), j - 16, row_of(j, core))


def put(ref, lead, rows, value):
    high, low = split(value)
    ref[lead + (pl.ds(0, rows),)] = high
    ref[lead + (pl.ds(rows, rows),)] = low


def select(taps, view, axis, index):
    total = jnp.zeros(index.shape, F32)
    for k in range(TAPS):
        total = jnp.where(index == k, taps[(view * 3 + axis) * TAPS + k], total)
    return total


def in_grid(slot, plane, tile):
    at = plane + W * tile
    return (slot < 46) & (at >= 0) & (at < 1024)


def matrices_kernel(where, taps, xf, yf, yt, zf, zt):
    core, tile = where[0], where[1]

    shape = (VIEWS * W, 2 * SLOTS)
    slot = iota(shape, 1)
    slot = jnp.where(slot < SLOTS, slot, slot - SLOTS)
    plane = plane_of(slot, core)
    row = iota(shape, 0)
    index = jnp.where(in_grid(slot, plane, tile), plane - row % W + REACH, -1)
    total = jnp.zeros(shape, F32)
    for view in range(VIEWS):
        total = jnp.where(row // W == view, select(taps, view, 0, index), total)
    put(xf, (), VIEWS * W, total)

    def per_view(view, _):
        shape = (MID, 2 * EXT)
        j = iota(shape, 1)
        j = jnp.where(j < EXT, j, j - EXT)
        index = row_of(j, core) - mid_row_of(iota(shape, 0), core) + REACH
        put(yf, (view,), MID, select(taps, view, 1, index))
        shape = (HALF, 2 * MID)
        j = iota(shape, 1)
        j = jnp.where(j < MID, j, j - MID)
        index = row_of(iota(shape, 0), core) - mid_row_of(j, core) + REACH
        put(yt, (view,), HALF, select(taps, view, 1, index))
        difference = iota((NZ, NZ), 0) - iota((NZ, NZ), 1)
        for ref, sign in ((zf, 1), (zt, -1)):
            high, low = split(select(taps, view, 2, sign * difference + REACH))
            for start in (0, NZ):
                ref[view, pl.ds(start, NZ), pl.ds(0, NZ)] = high
                ref[view, pl.ds(start, NZ), pl.ds(NZ, NZ)] = low
        return 0

    lax.fori_loop(0, VIEWS, per_view, 0)


def make_matrices(where, taps):
    shapes = [
        (2 * VIEWS * W, 2 * SLOTS),
        (VIEWS, 2 * MID, 2 * EXT),
        (VIEWS, 2 * HALF, 2 * MID),
        (VIEWS, 2 * NZ, 2 * NZ),
        (VIEWS, 2 * NZ, 2 * NZ),
    ]
    return pl.pallas_call(
        matrices_kernel,
        out_shape=[jax.ShapeDtypeStruct(s, BF16) for s in shapes],
        in_specs=[SMEM, SMEM],
        out_specs=[VMEM] * 5,
        compiler_params=pltpu.CompilerParams(vmem_limit_bytes=6 << 20),
        cost_estimate=pl.CostEstimate(flops=6_000_000_000, bytes_accessed=6_000_000, transcendentals=0),
        name="matrices",
    )(where, taps)


def cover_kernel(where, taps, cover, xt):
    core, tile = where[0], where[1]
    shape = (SLOTS, 2 * VIEWS * W)
    slot = iota(shape, 0)
    plane = plane_of(slot, 1 - core)
    column = iota(shape, 1)
    column = jnp.where(column < VIEWS * W, column, column - VIEWS * W)
    index = jnp.where(in_grid(slot, plane, tile), plane - column % W + REACH, -1)
    total = jnp.zeros(shape, F32)
    for view in range(VIEWS):
        covered = jnp.zeros((SLOTS, 2 * VIEWS * W), F32)
        for p in range(3 * W):
            covered = jnp.where(plane == p - W, cover[(p // W) * VIEWS * W + view * W + p % W], covered)
        total = jnp.where(column // W == view, select(taps, view, 0, index) * covered, total)
    put(xt, (), SLOTS, total)


def cover_matrix(where, taps, cover):
    return pl.pallas_call(
        cover_kernel,
        out_shape=jax.ShapeDtypeStruct((2 * SLOTS, 2 * VIEWS * W), BF16),
        in_specs=[SMEM, SMEM, SMEM],
        out_specs=VMEM,
        compiler_params=pltpu.CompilerParams(vmem_limit_bytes=2 << 20),
        cost_estimate=pl.CostEstimate(flops=2_000_000_000, bytes_accessed=1_000_000, transcendentals=0),
        name="cover_matrix",
    )(where, taps, cover)


def both(result):
    half = result.shape[0] // 2
    return result[:half] + result[half:]


def pair(result):
    return result[:, :NZ] + result[:, NZ:]


def beside(blocks):
    return jnp.concatenate(blocks, 1)


def along_x(source, target, matrix, rows, taken, given, source_step, target_step):
    group = 16

    def body(step, _):
        parts = [split(source[pl.ds(step * group + i, taken, stride=source_step)]) for i in range(group)]
        operand = jnp.concatenate([beside([p[0] for p in parts]), beside([p[1] for p in parts])], 0)
        result = both(dot(matrix[...], operand))
        for i in range(group):
            target[pl.ds(step * group + i, given, stride=target_step)] = result[:, i * NZ : (i + 1) * NZ]
        return 0

    lax.fori_loop(0, rows // group, body, 0)


def place(ext, step, rows, sources):
    slot = 0
    for source in sources:
        for i in range(source.shape[0]):
            ext[pl.ds(slot * step, rows)] = source[i, pl.ds(0, rows)]
            slot += 1
    while slot < SLOTS:
        ext[pl.ds(slot * step, rows)] = jnp.zeros((rows, NZ), F32)
        slot += 1


def own_kernel(first, own, second, xf, zf, out_high, out_low, ext, mid):
    place(ext, OWN_STEP, HALF, (first, own, second))
    along_x(ext, mid, xf, HALF, SLOTS, VIEWS * W, OWN_STEP, OWN_STEP)

    def along_z(view, _):
        start = pl.multiple_of(view * (W * OWN_STEP), 16)
        block = jnp.concatenate([mid[pl.ds(start + i * OWN_STEP, HALF)] for i in range(W)], 0)
        high, low = split(pair(dot(beside(split(block)), zf[view])))
        for i in range(W):
            out_high[view * W + i] = high[i * HALF : (i + 1) * HALF]
            out_low[view * W + i] = low[i * HALF : (i + 1) * HALF]
        return 0

    lax.fori_loop(0, VIEWS, along_z, 0, unroll=3)


def blur_own(first, own, second, xf, zf):
    return pl.pallas_call(
        own_kernel,
        out_shape=[jax.ShapeDtypeStruct((VIEWS * W, HALF, NZ), BF16)] * 2,
        in_specs=[VMEM] * 5,
        out_specs=[VMEM] * 2,
        scratch_shapes=[pltpu.VMEM((SLOTS * OWN_STEP, NZ), F32), pltpu.VMEM((VIEWS * W * OWN_STEP, NZ), F32)],
        compiler_params=pltpu.CompilerParams(vmem_limit_bytes=14 << 20),
        cost_estimate=pl.CostEstimate(flops=20_000_000_000, bytes_accessed=6_000_000, transcendentals=0),
        name="blur_own",
    )(first, own, second, xf, zf)


def correct_kernel(
    own_high, own_low, other1, other2, other3, mine, theirs, xf, xt, yf, yt, zf, zt,
    out1, out_own, out2, ext, mid, back, wide,
):
    rest = EXT - HALF
    place(ext, OTHER_STEP, rest, (other1, other2, other3))
    along_x(ext, mid, xf, rest, SLOTS, VIEWS * W, OTHER_STEP, OTHER_STEP)

    def inner(data, base):
        def body(step, _):
            view = base + step
            start = pl.multiple_of(view * (W * OTHER_STEP), 16)
            block = jnp.concatenate([mid[pl.ds(start + i * OTHER_STEP, rest)] for i in range(W)], 0)
            parts = split(pair(dot(beside(split(block)), zf[view])))
            operand = jnp.concatenate(
                [
                    piece
                    for ref, part in zip((own_high, own_low), parts)
                    for piece in (
                        beside([ref[view * W + i] for i in range(W)]),
                        beside([part[i * rest : (i + 1) * rest] for i in range(W)]),
                    )
                ],
                0,
            )
            blurred = both(dot(yf[view], operand))
            measured = beside([data[step, i] for i in range(W)])
            result = both(dot(yt[view], jnp.concatenate(split(measured / blurred), 0)))
            block = jnp.concatenate([result[:, i * NZ : (i + 1) * NZ] for i in range(W)], 0)
            block = pair(dot(beside(split(block)), zt[view]))
            start = pl.multiple_of(view * (W * OWN_STEP), 16)
            for i in range(W):
                back[pl.ds(start + i * OWN_STEP, HALF)] = block[i * HALF : (i + 1) * HALF]
            return 0

        lax.fori_loop(0, VIEWS // 2, body, 0, unroll=3)

    inner(mine, 0)
    inner(theirs, VIEWS // 2)
    along_x(back, wide, xt, HALF, VIEWS * W, SLOTS, OWN_STEP, OWN_STEP)
    for i in range(15):
        out1[i] = wide[pl.ds(i * OWN_STEP, HALF)]
        out2[i] = wide[pl.ds((i + 31) * OWN_STEP, HALF)]
    for i in range(16):
        out_own[i] = wide[pl.ds((i + 15) * OWN_STEP, HALF)]


def correct(own_high, own_low, other1, other2, other3, mine, theirs, xf, xt, yf, yt, zf, zt):
    shapes = [(15, HALF, NZ), (16, HALF, NZ), (15, HALF, NZ)]
    return pl.pallas_call(
        correct_kernel,
        out_shape=[jax.ShapeDtypeStruct(s, F32) for s in shapes],
        in_specs=[VMEM] * 13,
        out_specs=[VMEM] * 3,
        scratch_shapes=[
            pltpu.VMEM((SLOTS * OTHER_STEP, NZ), F32),
            pltpu.VMEM((VIEWS * W * OTHER_STEP, NZ), F32),
            pltpu.VMEM((VIEWS * W * OWN_STEP, NZ), F32),
            pltpu.VMEM((SLOTS * OWN_STEP, NZ), F32),
        ],
        compiler_params=pltpu.CompilerParams(vmem_limit_bytes=28 << 20),
        cost_estimate=pl.CostEstimate(flops=4_000_000_000, bytes_accessed=16_000_000, transcendentals=0),
        name="correct",
    )(own_high, own_low, other1, other2, other3, mine, theirs, xf, xt, yf, yt, zf, zt)


def begin_kernel(where, estimate, current, send1, send2):
    core = where[0]
    near = pl.ds(pl.multiple_of(32 + 32 * core, 32), 32)
    far = pl.ds(pl.multiple_of(96 * core, 32), 32)
    for i in range(W):
        current[i, pl.ds(0, 32)] = estimate[i, near]
        current[i, pl.ds(32, 32)] = estimate[i, far]
    send1[...] = current[pl.ds(1 - core, 15)]
    send2[...] = current[pl.ds(core, 15)]


def begin(where, estimate):
    shapes = [(16, HALF, NZ), (15, HALF, NZ), (15, HALF, NZ)]
    return pl.pallas_call(
        begin_kernel,
        out_shape=[jax.ShapeDtypeStruct(s, F32) for s in shapes],
        in_specs=[SMEM, VMEM],
        out_specs=[VMEM] * 3,
        compiler_params=pltpu.CompilerParams(vmem_limit_bytes=6 << 20),
        cost_estimate=pl.CostEstimate(flops=1_000_000, bytes_accessed=4_000_000, transcendentals=0),
        name="begin",
    )(where, estimate)


def rows_kernel(where, data, mine, send):
    core = where[0]
    for ref, who in ((mine, core), (send, 1 - core)):
        for start, at, count in ((32 + 32 * who, 0, 32), (96 * who, 32, 32), (64 - 16 * who, 64, 16)):
            source = pl.ds(pl.multiple_of(start, 16), count)
            for view in range(VIEWS // 2):
                for i in range(W):
                    ref[view, i, pl.ds(at, count)] = data[view, i, source]


def rows(where, data):
    return pl.pallas_call(
        rows_kernel,
        out_shape=[jax.ShapeDtypeStruct((VIEWS // 2, W, MID, NZ), F32)] * 2,
        in_specs=[SMEM, VMEM],
        out_specs=[VMEM] * 2,
        compiler_params=pltpu.CompilerParams(vmem_limit_bytes=10 << 20),
        cost_estimate=pl.CostEstimate(flops=0, bytes_accessed=8_000_000, transcendentals=0),
        name="rows",
    )(where, data)


def update_kernel(where, keep, scale, current, total, from1, from2, new, send1, send2, work):
    core = where[0]
    work[...] = total[...]
    work[pl.ds(core, 15)] += from1[...]
    work[pl.ds(1 - core, 15)] += from2[...]
    for i in range(W):
        new[i] = current[i] * (work[i] + keep[i]) * scale[i]
    send1[...] = new[pl.ds(1 - core, 15)]
    send2[...] = new[pl.ds(core, 15)]


def update(where, keep, scale, current, total, from1, from2):
    shapes = [(16, HALF, NZ), (15, HALF, NZ), (15, HALF, NZ)]
    return pl.pallas_call(
        update_kernel,
        out_shape=[jax.ShapeDtypeStruct(s, F32) for s in shapes],
        in_specs=[SMEM] * 3 + [VMEM] * 4,
        out_specs=[VMEM] * 3,
        scratch_shapes=[pltpu.VMEM((16, HALF, NZ), F32)],
        compiler_params=pltpu.CompilerParams(vmem_limit_bytes=6 << 20),
        cost_estimate=pl.CostEstimate(flops=1_000_000, bytes_accessed=4_000_000, transcendentals=0),
        name="update",
    )(where, keep, scale, current, total, from1, from2)


def neighbours(x, up_core, tiles):
    pairs = []
    for t in range(tiles):
        pairs.append((2 * t + up_core, 2 * ((t + 1) % tiles) + up_core))
        pairs.append((2 * t + 1 - up_core, 2 * ((t - 1) % tiles) + 1 - up_core))
    return lax.ppermute(x, ("tile", "view"), pairs)


def swap(x):
    return lax.ppermute(x, "view", [(0, 1), (1, 0)])


def per_device(estimate, view_data, psf_taps, coverage):
    tiles = lax.axis_size("tile")
    core = lax.axis_index("view")
    tile = lax.axis_index("tile")
    where = jnp.stack([core, tile]).astype(jnp.int32)
    current, send1, send2 = begin(where, estimate)
    psf_taps, coverage, send1, send2 = lax.optimization_barrier((psf_taps, coverage, send1, send2))

    norm_taps = psf_taps / jnp.sum(psf_taps, axis=-1, keepdims=True)
    own = jnp.concatenate([norm_taps.reshape(-1), coverage.astype(F32).reshape(-1)])
    other, view_data = lax.optimization_barrier((swap(own), view_data))
    count = norm_taps.size
    taps = jnp.concatenate([own[:count], other[:count]])
    cover = jnp.concatenate([own[count:], other[count:]])
    ring = [(i, (i + 1) % tiles) for i in range(tiles)]
    before = lax.ppermute(cover, "tile", ring)
    after = lax.ppermute(cover, "tile", [(j, i) for i, j in ring])
    seen = jnp.sum(cover.reshape(VIEWS, W), axis=0)
    keep = 1.0 - jnp.minimum(seen, 1.0)
    scale = 1.0 / jnp.maximum(seen, 1.0)
    mine, theirs = rows(where, view_data)
    theirs = swap(theirs)
    xf, yf, yt, zf, zt = make_matrices(where, taps)
    xt = cover_matrix(where, taps, jnp.concatenate([before, cover, after]))

    for iteration in range(ITERS):
        first = neighbours(send1, 0, tiles)
        second = neighbours(send2, 1, tiles)
        high, low = blur_own(first, current, second, xf, zf)
        spread1, total, spread2 = correct(
            high, low, swap(second), swap(current), swap(first), mine, theirs, xf, xt, yf, yt, zf, zt
        )
        from1 = neighbours(spread1, 0, tiles)
        from2 = neighbours(spread2, 1, tiles)
        current, send1, send2 = update(where, keep, scale, current, total, from1, from2)

    other = swap(current)
    low = jnp.where(core == 0, current, other)
    high = jnp.where(core == 0, other, current)
    return jnp.concatenate([low[:, 32:], low[:, :32], high[:, :32], high[:, 32:]], 1)


def solution(mesh):
    return jax.shard_map(
        per_device,
        mesh=mesh,
        in_specs=(
            P("tile", None, None),
            P("view", "tile", None, None),
            P("view", None, None),
            P("view", "tile"),
        ),
        out_specs=P("tile", None, None),
        check_vma=False,
    )
```

```python
import functools

import jax
import jax.numpy as jnp
from jax import lax
from jax.experimental import pallas as pl
from jax.experimental.pallas import tpu as pltpu
from jax.sharding import PartitionSpec as P

ITERS = 4
TAPS = 31
REACH = 15
VIEWS = 6
W = 16
HALF = 64
EXT = 96
MID = 80
SLOTS = 48
NZ = 128
PART = 32
OWN_STEP = 65
PART_STEP = 33
F32 = jnp.float32
BF16 = jnp.bfloat16
VMEM = pl.BlockSpec(memory_space=pltpu.VMEM)
SMEM = pl.BlockSpec(memory_space=pltpu.SMEM)


def split(x):
    high = x.astype(BF16)
    return high, (x - high.astype(F32)).astype(BF16)


def dot(a, b):
    return jnp.dot(a, b, preferred_element_type=F32)


def iota(shape, dim):
    return lax.broadcasted_iota(jnp.int32, shape, dim)


def plane_of(slot, odd):
    middle = slot - REACH
    swapped = jnp.where(slot < REACH, slot + W, jnp.where(slot < REACH + W, middle, slot - 46))
    return jnp.where(odd == 0, middle, swapped)


def row_of(j, core):
    first = jnp.where(j < 32, j + 32, jnp.where(j < 64, j - 32, j))
    second = jnp.where(j < 64, j + 64, j - 32)
    return jnp.where(core == 0, first, second)


def mid_row_of(j, core):
    return jnp.where((core == 1) & (j >= 64), j - 16, row_of(j, core))


def put(ref, lead, rows, value):
    high, low = split(value)
    ref[lead + (pl.ds(0, rows),)] = high
    ref[lead + (pl.ds(rows, rows),)] = low


def select(taps, view, axis, index):
    total = jnp.zeros(index.shape, F32)
    for k in range(TAPS):
        total = jnp.where(index == k, taps[(view * 3 + axis) * TAPS + k], total)
    return total


def in_grid(slot, plane, tile):
    at = plane + W * tile
    return (slot < 46) & (at >= 0) & (at < 1024)


def matrices_kernel(where, taps, xf, yf, yt, zf, zt):
    core, tile, odd = where[0], where[1], where[2]

    shape = (VIEWS * W, 2 * SLOTS)
    slot = iota(shape, 1)
    slot = jnp.where(slot < SLOTS, slot, slot - SLOTS)
    plane = plane_of(slot, odd)
    row = iota(shape, 0)
    index = jnp.where(in_grid(slot, plane, tile), plane - row % W + REACH, -1)
    total = jnp.zeros(shape, F32)
    for view in range(VIEWS):
        total = jnp.where(row // W == view, select(taps, view, 0, index), total)
    put(xf, (), VIEWS * W, total)

    def per_view(view, _):
        shape = (MID, 2 * EXT)
        j = iota(shape, 1)
        j = jnp.where(j < EXT, j, j - EXT)
        index = row_of(j, core) - mid_row_of(iota(shape, 0), core) + REACH
        put(yf, (view,), MID, select(taps, view, 1, index))
        shape = (HALF, 2 * MID)
        j = iota(shape, 1)
        j = jnp.where(j < MID, j, j - MID)
        index = row_of(iota(shape, 0), core) - mid_row_of(j, core) + REACH
        put(yt, (view,), HALF, select(taps, view, 1, index))
        difference = iota((NZ, NZ), 0) - iota((NZ, NZ), 1)
        for ref, sign in ((zf, 1), (zt, -1)):
            high, low = split(select(taps, view, 2, sign * difference + REACH))
            for start in (0, NZ):
                ref[view, pl.ds(start, NZ), pl.ds(0, NZ)] = high
                ref[view, pl.ds(start, NZ), pl.ds(NZ, NZ)] = low
        return 0

    lax.fori_loop(0, VIEWS, per_view, 0)


def make_matrices(where, taps):
    shapes = [
        (2 * VIEWS * W, 2 * SLOTS),
        (VIEWS, 2 * MID, 2 * EXT),
        (VIEWS, 2 * HALF, 2 * MID),
        (VIEWS, 2 * NZ, 2 * NZ),
        (VIEWS, 2 * NZ, 2 * NZ),
    ]
    return pl.pallas_call(
        matrices_kernel,
        out_shape=[jax.ShapeDtypeStruct(s, BF16) for s in shapes],
        in_specs=[SMEM, SMEM],
        out_specs=[VMEM] * 5,
        compiler_params=pltpu.CompilerParams(vmem_limit_bytes=6 << 20),
        cost_estimate=pl.CostEstimate(flops=1_000, bytes_accessed=1_000, transcendentals=0),
        name="matrices",
    )(where, taps)


def cover_kernel(where, taps, cover, xt):
    core, tile, odd = where[0], where[1], where[2]
    shape = (SLOTS, 2 * VIEWS * W)
    slot = iota(shape, 0)
    plane = plane_of(slot, odd)
    column = iota(shape, 1)
    column = jnp.where(column < VIEWS * W, column, column - VIEWS * W)
    index = jnp.where(in_grid(slot, plane, tile), plane - column % W + REACH, -1)
    total = jnp.zeros(shape, F32)
    for view in range(VIEWS):
        covered = jnp.zeros((SLOTS, 2 * VIEWS * W), F32)
        for p in range(3 * W):
            covered = jnp.where(plane == p - W, cover[(p // W) * VIEWS * W + view * W + p % W], covered)
        total = jnp.where(column // W == view, select(taps, view, 0, index) * covered, total)
    put(xt, (), SLOTS, total)


def cover_matrix(where, taps, cover):
    return pl.pallas_call(
        cover_kernel,
        out_shape=jax.ShapeDtypeStruct((2 * SLOTS, 2 * VIEWS * W), BF16),
        in_specs=[SMEM, SMEM, SMEM],
        out_specs=VMEM,
        compiler_params=pltpu.CompilerParams(vmem_limit_bytes=2 << 20),
        cost_estimate=pl.CostEstimate(flops=1_000, bytes_accessed=1_000, transcendentals=0),
        name="cover_matrix",
    )(where, taps, cover)


def both(result):
    half = result.shape[0] // 2
    return result[:half] + result[half:]


def pair(result):
    return result[:, :NZ] + result[:, NZ:]


def beside(blocks):
    return jnp.concatenate(blocks, 1)


def along_x(source, target, matrix, rows, taken, given, source_step, target_step):
    group = 16

    def body(step, _):
        parts = [split(source[pl.ds(step * group + i, taken, stride=source_step)]) for i in range(group)]
        operand = jnp.concatenate([beside([p[0] for p in parts]), beside([p[1] for p in parts])], 0)
        result = both(dot(matrix[...], operand))
        for i in range(group):
            target[pl.ds(step * group + i, given, stride=target_step)] = result[:, i * NZ : (i + 1) * NZ]
        return 0

    lax.fori_loop(0, rows // group, body, 0)


def blur_kernel(at, first, own, second, xf, zf, out_high, out_low, ext, mid):
    slot = 0
    for source in (first, own, second):
        for i in range(source.shape[0]):
            ext[pl.ds(slot * PART_STEP, PART)] = source[i, pl.ds(at, PART)]
            slot += 1
    while slot < SLOTS:
        ext[pl.ds(slot * PART_STEP, PART)] = jnp.zeros((PART, NZ), F32)
        slot += 1
    along_x(ext, mid, xf, PART, SLOTS, VIEWS * W, PART_STEP, PART_STEP)

    def along_z(view, _):
        start = pl.multiple_of(view * (W * PART_STEP), 16)
        block = jnp.concatenate([mid[pl.ds(start + i * PART_STEP, PART)] for i in range(W)], 0)
        high, low = split(pair(dot(beside(split(block)), zf[view])))
        for i in range(W):
            out_high[view * W + i] = high[i * PART : (i + 1) * PART]
            out_low[view * W + i] = low[i * PART : (i + 1) * PART]
        return 0

    lax.fori_loop(0, VIEWS, along_z, 0, unroll=3)


def blur(first, own, second, xf, zf, at=0):
    return pl.pallas_call(
        functools.partial(blur_kernel, at),
        out_shape=[jax.ShapeDtypeStruct((VIEWS * W, PART, NZ), BF16)] * 2,
        in_specs=[VMEM] * 5,
        out_specs=[VMEM] * 2,
        scratch_shapes=[pltpu.VMEM((SLOTS * PART_STEP, NZ), F32), pltpu.VMEM((VIEWS * W * PART_STEP, NZ), F32)],
        compiler_params=pltpu.CompilerParams(vmem_limit_bytes=10 << 20),
        cost_estimate=pl.CostEstimate(flops=10_000_000_000, bytes_accessed=3_000_000, transcendentals=0),
        name="blur",
    )(first, own, second, xf, zf)


def correct_kernel(
    near_high, near_low, far_high, far_low, other_high, other_low, mine, theirs, xt, yf, yt, zt,
    near1, near_own, near2, far1, far_own, far2, back, wide,
):
    blurs = ((near_high, far_high, other_high), (near_low, far_low, other_low))

    def inner(data, base):
        def body(step, _):
            view = base + step
            operand = jnp.concatenate(
                [beside([ref[view * W + i] for i in range(W)]) for refs in blurs for ref in refs], 0
            )
            blurred = both(dot(yf[view], operand))
            measured = beside([data[step, i] for i in range(W)])
            result = both(dot(yt[view], jnp.concatenate(split(measured / blurred), 0)))
            block = jnp.concatenate([result[:, i * NZ : (i + 1) * NZ] for i in range(W)], 0)
            block = pair(dot(beside(split(block)), zt[view]))
            start = pl.multiple_of(view * (W * OWN_STEP), 16)
            for i in range(W):
                back[pl.ds(start + i * OWN_STEP, HALF)] = block[i * HALF : (i + 1) * HALF]
            return 0

        lax.fori_loop(0, VIEWS // 2, body, 0, unroll=3)

    inner(mine, 0)
    inner(theirs, VIEWS // 2)
    along_x(back, wide, xt, HALF, VIEWS * W, SLOTS, OWN_STEP, OWN_STEP)
    for at, outs in ((0, (near1, near_own, near2)), (PART, (far1, far_own, far2))):
        for slot, out in zip((0, 15, 31), outs):
            for i in range(out.shape[0]):
                out[i] = wide[pl.ds((slot + i) * OWN_STEP + at, PART)]


PARTS = [(15, PART, NZ), (16, PART, NZ), (15, PART, NZ)]


def correct(blurs, mine, theirs, xt, yf, yt, zt):
    return pl.pallas_call(
        correct_kernel,
        out_shape=[jax.ShapeDtypeStruct(s, F32) for s in PARTS * 2],
        in_specs=[VMEM] * 12,
        out_specs=[VMEM] * 6,
        scratch_shapes=[
            pltpu.VMEM((VIEWS * W * OWN_STEP, NZ), F32),
            pltpu.VMEM((SLOTS * OWN_STEP, NZ), F32),
        ],
        compiler_params=pltpu.CompilerParams(vmem_limit_bytes=26 << 20),
        cost_estimate=pl.CostEstimate(flops=4_000_000_000, bytes_accessed=16_000_000, transcendentals=0),
        name="correct",
    )(*blurs, mine, theirs, xt, yf, yt, zt)


def begin_kernel(where, estimate, current, send1, send2):
    core, odd = where[0], where[2]
    for start, at in ((32 + 32 * core, 0), (96 * core, PART)):
        rows = pl.ds(pl.multiple_of(start, 32), PART)
        for i in range(W):
            current[i, pl.ds(at, PART)] = estimate[i, rows]
    send1[...] = current[pl.ds(odd, 15)]
    send2[...] = current[pl.ds(1 - odd, 15)]


def begin(where, estimate):
    shapes = [(16, HALF, NZ), (15, HALF, NZ), (15, HALF, NZ)]
    return pl.pallas_call(
        begin_kernel,
        out_shape=[jax.ShapeDtypeStruct(s, F32) for s in shapes],
        in_specs=[SMEM, VMEM],
        out_specs=[VMEM] * 3,
        compiler_params=pltpu.CompilerParams(vmem_limit_bytes=6 << 20),
        cost_estimate=pl.CostEstimate(flops=1_000, bytes_accessed=1_000, transcendentals=0),
        name="begin",
    )(where, estimate)


def rows_kernel(where, data, mine, send):
    core = where[0]
    for ref, who in ((mine, core), (send, 1 - core)):
        for start, at, count in ((32 + 32 * who, 0, 32), (96 * who, 32, 32), (64 - 16 * who, 64, 16)):
            source = pl.ds(pl.multiple_of(start, 16), count)
            for view in range(VIEWS // 2):
                for i in range(W):
                    ref[view, i, pl.ds(at, count)] = data[view, i, source]


def rows(where, data):
    return pl.pallas_call(
        rows_kernel,
        out_shape=[jax.ShapeDtypeStruct((VIEWS // 2, W, MID, NZ), F32)] * 2,
        in_specs=[SMEM, VMEM],
        out_specs=[VMEM] * 2,
        compiler_params=pltpu.CompilerParams(vmem_limit_bytes=10 << 20),
        cost_estimate=pl.CostEstimate(flops=1_000, bytes_accessed=1_000, transcendentals=0),
        name="rows",
    )(where, data)


def add_neighbours(where, keep, scale, current, total, from1, from2, new, work):
    odd = where[2]
    work[...] = total[...]
    work[pl.ds(odd, 15)] += from1[...]
    work[pl.ds(1 - odd, 15)] += from2[...]
    for i in range(W):
        new[i] = current[i] * (work[i] + keep[i]) * scale[i]


def update_kernel(where, keep, scale, current, total, from1, from2, new, send1, send2, work):
    odd = where[2]
    add_neighbours(where, keep, scale, current, total, from1, from2, new, work)
    send1[...] = new[pl.ds(odd, 15)]
    send2[...] = new[pl.ds(1 - odd, 15)]


def update(where, keep, scale, current, total, from1, from2, last):
    shapes = [PARTS[1]] if last else [PARTS[1], PARTS[0], PARTS[2]]
    return pl.pallas_call(
        add_neighbours if last else update_kernel,
        out_shape=[jax.ShapeDtypeStruct(s, F32) for s in shapes],
        in_specs=[SMEM] * 3 + [VMEM] * 4,
        out_specs=[VMEM] * len(shapes),
        scratch_shapes=[pltpu.VMEM(PARTS[1], F32)],
        compiler_params=pltpu.CompilerParams(vmem_limit_bytes=4 << 20),
        cost_estimate=pl.CostEstimate(flops=1_000_000, bytes_accessed=2_000_000, transcendentals=0),
        name="update",
    )(where, keep, scale, current, total, from1, from2)


def exchange(x, odd, tiles):
    pairs = []
    for t in range(odd, tiles, 2):
        pairs += [(t, (t + 1) % tiles), ((t + 1) % tiles, t)]
    return lax.ppermute(x, "tile", pairs)


def swap(x):
    return lax.ppermute(x, "view", [(0, 1), (1, 0)])


def per_device(estimate, view_data, psf_taps, coverage):
    tiles = lax.axis_size("tile")
    core = lax.axis_index("view")
    tile = lax.axis_index("tile")
    where = jnp.stack([core, tile, tile % 2]).astype(jnp.int32)
    current, send1, send2 = begin(where, estimate)
    other_current = swap(current)
    psf_taps, coverage, send1, send2 = lax.optimization_barrier((psf_taps, coverage, send1, send2))

    norm_taps = psf_taps / jnp.sum(psf_taps, axis=-1, keepdims=True)
    own = jnp.concatenate([norm_taps.reshape(-1), coverage.astype(F32).reshape(-1)])
    other, view_data = lax.optimization_barrier((swap(own), view_data))
    count = norm_taps.size
    taps = jnp.concatenate([own[:count], other[:count]])
    cover = jnp.concatenate([own[count:], other[count:]])
    ring = [(i, (i + 1) % tiles) for i in range(tiles)]
    before = lax.ppermute(cover, "tile", ring)
    after = lax.ppermute(cover, "tile", [(j, i) for i, j in ring])
    seen = jnp.sum(cover.reshape(VIEWS, W), axis=0)
    keep = 1.0 - jnp.minimum(seen, 1.0)
    scale = 1.0 / jnp.maximum(seen, 1.0)
    mine, theirs = rows(where, view_data)
    theirs = swap(theirs)
    xf, yf, yt, zf, zt = make_matrices(where, taps)
    xt = cover_matrix(where, taps, jnp.concatenate([before, cover, after]))

    for iteration in range(ITERS):
        last = iteration == ITERS - 1
        if iteration == 0:
            send1, send2 = exchange(send1, 1, tiles), exchange(send2, 0, tiles)
            others = blur(swap(send1), other_current, swap(send2), xf, zf)
            blurs = blur(send1, current, send2, xf, zf) + blur(send1, current, send2, xf, zf, PART)
            near, far = current[:, :PART], current[:, PART:]
        else:
            near1, near2 = exchange(near1, 1, tiles), exchange(near2, 0, tiles)
            far1, far2 = exchange(far1, 1, tiles), exchange(far2, 0, tiles)
            blurs = blur(near1, near, near2, xf, zf)
            others = blur(swap(near1), swap(near), swap(near2), xf, zf)
            far, others = lax.optimization_barrier((far, others))
            blurs = blurs + blur(far1, far, far2, xf, zf)
        near1, near_total, near2, far1, far_total, far2 = correct(blurs + others, mine, theirs, xt, yf, yt, zt)
        near1, near2 = exchange(near1, 1, tiles), exchange(near2, 0, tiles)
        far1, far2 = exchange(far1, 1, tiles), exchange(far2, 0, tiles)
        near, *sends = update(where, keep, scale, near, near_total, near1, near2, last)
        if not last:
            near1, near2 = sends
        far1, far2, near = lax.optimization_barrier((far1, far2, near))
        far, *sends = update(where, keep, scale, far, far_total, far1, far2, last)
        if not last:
            far1, far2 = sends

    zero = core == 0
    other_near, other_far = swap(near), swap(far)
    return jnp.concatenate(
        [
            jnp.where(zero, far, other_far),
            jnp.where(zero, near, other_near),
            jnp.where(zero, other_near, near),
            jnp.where(zero, other_far, far),
        ],
        1,
    )


def solution(mesh):
    return jax.shard_map(
        per_device,
        mesh=mesh,
        in_specs=(
            P("tile", None, None),
            P("view", "tile", None, None),
            P("view", None, None),
            P("view", "tile"),
        ),
        out_specs=P("tile", None, None),
        check_vma=False,
    )
```

```python
import functools

import jax
import jax.numpy as jnp
from jax import lax
from jax.experimental import pallas as pl
from jax.experimental.pallas import tpu as pltpu
from jax.sharding import PartitionSpec as P

ITERS = 4
TAPS = 31
REACH = 15
VIEWS = 6
W = 16
HALF = 64
EXT = 96
MID = 80
SLOTS = 48
NZ = 128
PART = 32
OWN_STEP = 65
PART_STEP = 33
F32 = jnp.float32
BF16 = jnp.bfloat16
VMEM = pl.BlockSpec(memory_space=pltpu.VMEM)
SMEM = pl.BlockSpec(memory_space=pltpu.SMEM)


def split(x):
    high = x.astype(BF16)
    return high, (x - high.astype(F32)).astype(BF16)


def dot(a, b):
    return jnp.dot(a, b, preferred_element_type=F32)


def iota(shape, dim):
    return lax.broadcasted_iota(jnp.int32, shape, dim)


def plane_of(slot, odd):
    middle = slot - REACH
    swapped = jnp.where(slot < REACH, slot + W, jnp.where(slot < REACH + W, middle, slot - 46))
    return jnp.where(odd == 0, middle, swapped)


def row_of(j, core):
    first = jnp.where(j < 32, j + 32, jnp.where(j < 64, j - 32, j))
    second = jnp.where(j < 64, j + 64, j - 32)
    return jnp.where(core == 0, first, second)


def mid_row_of(j, core):
    return jnp.where((core == 1) & (j >= 64), j - 16, row_of(j, core))


def put(ref, lead, rows, value):
    high, low = split(value)
    ref[lead + (pl.ds(0, rows),)] = high
    ref[lead + (pl.ds(rows, rows),)] = low


def select(taps, view, axis, index):
    total = jnp.zeros(index.shape, F32)
    for k in range(TAPS):
        total = jnp.where(index == k, taps[(view * 3 + axis) * TAPS + k], total)
    return total


def in_grid(slot, plane, tile):
    at = plane + W * tile
    return (slot < 46) & (at >= 0) & (at < 1024)


def matrices_kernel(where, taps, xf, yf, yt, zf, zt):
    core, tile, odd = where[0], where[1], where[2]

    shape = (VIEWS * W, 2 * SLOTS)
    slot = iota(shape, 1)
    slot = jnp.where(slot < SLOTS, slot, slot - SLOTS)
    plane = plane_of(slot, odd)
    row = iota(shape, 0)
    index = jnp.where(in_grid(slot, plane, tile), plane - row % W + REACH, -1)
    total = jnp.zeros(shape, F32)
    for view in range(VIEWS):
        total = jnp.where(row // W == view, select(taps, view, 0, index), total)
    put(xf, (), VIEWS * W, total)

    def per_view(view, _):
        shape = (MID, 2 * EXT)
        j = iota(shape, 1)
        j = jnp.where(j < EXT, j, j - EXT)
        index = row_of(j, core) - mid_row_of(iota(shape, 0), core) + REACH
        put(yf, (view,), MID, select(taps, view, 1, index))
        shape = (HALF, 2 * MID)
        j = iota(shape, 1)
        j = jnp.where(j < MID, j, j - MID)
        index = row_of(iota(shape, 0), core) - mid_row_of(j, core) + REACH
        put(yt, (view,), HALF, select(taps, view, 1, index))
        difference = iota((NZ, NZ), 0) - iota((NZ, NZ), 1)
        for ref, sign in ((zf, 1), (zt, -1)):
            high, low = split(select(taps, view, 2, sign * difference + REACH))
            for start in (0, NZ):
                ref[view, pl.ds(start, NZ), pl.ds(0, NZ)] = high
                ref[view, pl.ds(start, NZ), pl.ds(NZ, NZ)] = low
        return 0

    lax.fori_loop(0, VIEWS, per_view, 0)


def make_matrices(where, taps):
    shapes = [
        (2 * VIEWS * W, 2 * SLOTS),
        (VIEWS, 2 * MID, 2 * EXT),
        (VIEWS, 2 * HALF, 2 * MID),
        (VIEWS, 2 * NZ, 2 * NZ),
        (VIEWS, 2 * NZ, 2 * NZ),
    ]
    return pl.pallas_call(
        matrices_kernel,
        out_shape=[jax.ShapeDtypeStruct(s, BF16) for s in shapes],
        in_specs=[SMEM, SMEM],
        out_specs=[VMEM] * 5,
        compiler_params=pltpu.CompilerParams(vmem_limit_bytes=6 << 20),
        cost_estimate=pl.CostEstimate(flops=1_000, bytes_accessed=1_000, transcendentals=0),
        name="matrices",
    )(where, taps)


def cover_kernel(where, taps, cover, xt):
    core, tile, odd = where[0], where[1], where[2]
    shape = (SLOTS, 2 * VIEWS * W)
    slot = iota(shape, 0)
    plane = plane_of(slot, odd)
    column = iota(shape, 1)
    column = jnp.where(column < VIEWS * W, column, column - VIEWS * W)
    index = jnp.where(in_grid(slot, plane, tile), plane - column % W + REACH, -1)
    total = jnp.zeros(shape, F32)
    for view in range(VIEWS):
        covered = jnp.zeros((SLOTS, 2 * VIEWS * W), F32)
        for p in range(3 * W):
            covered = jnp.where(plane == p - W, cover[(p // W) * VIEWS * W + view * W + p % W], covered)
        total = jnp.where(column // W == view, select(taps, view, 0, index) * covered, total)
    put(xt, (), SLOTS, total)


def cover_matrix(where, taps, cover):
    return pl.pallas_call(
        cover_kernel,
        out_shape=jax.ShapeDtypeStruct((2 * SLOTS, 2 * VIEWS * W), BF16),
        in_specs=[SMEM, SMEM, SMEM],
        out_specs=VMEM,
        compiler_params=pltpu.CompilerParams(vmem_limit_bytes=2 << 20),
        cost_estimate=pl.CostEstimate(flops=1_000, bytes_accessed=1_000, transcendentals=0),
        name="cover_matrix",
    )(where, taps, cover)


def both(result):
    half = result.shape[0] // 2
    return result[:half] + result[half:]


def pair(result):
    return result[:, :NZ] + result[:, NZ:]


def beside(blocks):
    return jnp.concatenate(blocks, 1)


def along_x(source, target, matrix, rows, taken, given, source_step, target_step):
    group = 16

    def body(step, _):
        parts = [split(source[pl.ds(step * group + i, taken, stride=source_step)]) for i in range(group)]
        operand = jnp.concatenate([beside([p[0] for p in parts]), beside([p[1] for p in parts])], 0)
        result = both(dot(matrix[...], operand))
        for i in range(group):
            target[pl.ds(step * group + i, given, stride=target_step)] = result[:, i * NZ : (i + 1) * NZ]
        return 0

    lax.fori_loop(0, rows // group, body, 0)


def blur_kernel(at, first, own, second, xf, zf, out_high, out_low, ext, mid):
    slot = 0
    for source in (first, own, second):
        for i in range(source.shape[0]):
            ext[pl.ds(slot * PART_STEP, PART)] = source[i, pl.ds(at, PART)]
            slot += 1
    while slot < SLOTS:
        ext[pl.ds(slot * PART_STEP, PART)] = jnp.zeros((PART, NZ), F32)
        slot += 1
    along_x(ext, mid, xf, PART, SLOTS, VIEWS * W, PART_STEP, PART_STEP)

    def along_z(view, _):
        start = pl.multiple_of(view * (W * PART_STEP), 16)
        block = jnp.concatenate([mid[pl.ds(start + i * PART_STEP, PART)] for i in range(W)], 0)
        high, low = split(pair(dot(beside(split(block)), zf[view])))
        for i in range(W):
            out_high[view * W + i] = high[i * PART : (i + 1) * PART]
            out_low[view * W + i] = low[i * PART : (i + 1) * PART]
        return 0

    lax.fori_loop(0, VIEWS, along_z, 0, unroll=3)


def blur(first, own, second, xf, zf, at=0):
    return pl.pallas_call(
        functools.partial(blur_kernel, at),
        out_shape=[jax.ShapeDtypeStruct((VIEWS * W, PART, NZ), BF16)] * 2,
        in_specs=[VMEM] * 5,
        out_specs=[VMEM] * 2,
        scratch_shapes=[pltpu.VMEM((SLOTS * PART_STEP, NZ), F32), pltpu.VMEM((VIEWS * W * PART_STEP, NZ), F32)],
        compiler_params=pltpu.CompilerParams(vmem_limit_bytes=10 << 20),
        cost_estimate=pl.CostEstimate(flops=10_000_000_000, bytes_accessed=3_000_000, transcendentals=0),
        name="blur",
    )(first, own, second, xf, zf)


def correct_kernel(
    near_high, near_low, far_high, far_low, other_high, other_low, mine, theirs, xt, yf, yt, zt,
    near1, near_own, near2, far1, far_own, far2, back, wide,
):
    blurs = ((near_high, far_high, other_high), (near_low, far_low, other_low))

    def inner(data, base, unroll):
        def body(step, _):
            view = base + step
            operand = jnp.concatenate(
                [beside([ref[view * W + i] for i in range(W)]) for refs in blurs for ref in refs], 0
            )
            blurred = both(dot(yf[view], operand))
            measured = beside([data[step, i] for i in range(W)])
            result = both(dot(yt[view], jnp.concatenate(split(measured / blurred), 0)))
            block = jnp.concatenate([result[:, i * NZ : (i + 1) * NZ] for i in range(W)], 0)
            block = pair(dot(beside(split(block)), zt[view]))
            start = pl.multiple_of(view * (W * OWN_STEP), 16)
            for i in range(W):
                back[pl.ds(start + i * OWN_STEP, HALF)] = block[i * HALF : (i + 1) * HALF]
            return 0

        lax.fori_loop(0, VIEWS // 2, body, 0, unroll=unroll)

    inner(mine, 0, 3)
    inner(theirs, VIEWS // 2, 1)
    along_x(back, wide, xt, HALF, VIEWS * W, SLOTS, OWN_STEP, OWN_STEP)
    for at, outs in ((0, (near1, near_own, near2)), (PART, (far1, far_own, far2))):
        for slot, out in zip((0, 15, 31), outs):
            for i in range(out.shape[0]):
                out[i] = wide[pl.ds((slot + i) * OWN_STEP + at, PART)]


PARTS = [(15, PART, NZ), (16, PART, NZ), (15, PART, NZ)]


def correct(blurs, mine, theirs, xt, yf, yt, zt):
    return pl.pallas_call(
        correct_kernel,
        out_shape=[jax.ShapeDtypeStruct(s, F32) for s in PARTS * 2],
        in_specs=[VMEM] * 12,
        out_specs=[VMEM] * 6,
        scratch_shapes=[
            pltpu.VMEM((VIEWS * W * OWN_STEP, NZ), F32),
            pltpu.VMEM((SLOTS * OWN_STEP, NZ), F32),
        ],
        compiler_params=pltpu.CompilerParams(vmem_limit_bytes=26 << 20),
        cost_estimate=pl.CostEstimate(flops=4_000_000_000, bytes_accessed=16_000_000, transcendentals=0),
        name="correct",
    )(*blurs, mine, theirs, xt, yf, yt, zt)


def begin_kernel(where, estimate, current, send1, send2):
    core, odd = where[0], where[2]
    for start, at in ((32 + 32 * core, 0), (96 * core, PART)):
        rows = pl.ds(pl.multiple_of(start, 32), PART)
        for i in range(W):
            current[i, pl.ds(at, PART)] = estimate[i, rows]
    send1[...] = current[pl.ds(odd, 15)]
    send2[...] = current[pl.ds(1 - odd, 15)]


def begin(where, estimate):
    shapes = [(16, HALF, NZ), (15, HALF, NZ), (15, HALF, NZ)]
    return pl.pallas_call(
        begin_kernel,
        out_shape=[jax.ShapeDtypeStruct(s, F32) for s in shapes],
        in_specs=[SMEM, VMEM],
        out_specs=[VMEM] * 3,
        compiler_params=pltpu.CompilerParams(vmem_limit_bytes=6 << 20),
        cost_estimate=pl.CostEstimate(flops=1_000, bytes_accessed=1_000, transcendentals=0),
        name="begin",
    )(where, estimate)


def rows_kernel(where, data, mine, send):
    core = where[0]
    for ref, who in ((mine, core), (send, 1 - core)):
        for start, at, count in ((32 + 32 * who, 0, 32), (96 * who, 32, 32), (64 - 16 * who, 64, 16)):
            source = pl.ds(pl.multiple_of(start, 16), count)
            for view in range(VIEWS // 2):
                for i in range(W):
                    ref[view, i, pl.ds(at, count)] = data[view, i, source]


def rows(where, data):
    return pl.pallas_call(
        rows_kernel,
        out_shape=[jax.ShapeDtypeStruct((VIEWS // 2, W, MID, NZ), F32)] * 2,
        in_specs=[SMEM, VMEM],
        out_specs=[VMEM] * 2,
        compiler_params=pltpu.CompilerParams(vmem_limit_bytes=10 << 20),
        cost_estimate=pl.CostEstimate(flops=1_000, bytes_accessed=1_000, transcendentals=0),
        name="rows",
    )(where, data)


def add_neighbours(where, keep, scale, current, total, from1, from2, new, work):
    odd = where[2]
    work[...] = total[...]
    work[pl.ds(odd, 15)] += from1[...]
    work[pl.ds(1 - odd, 15)] += from2[...]
    for i in range(W):
        new[i] = current[i] * (work[i] + keep[i]) * scale[i]


def update_kernel(where, keep, scale, current, total, from1, from2, new, send1, send2, work):
    odd = where[2]
    add_neighbours(where, keep, scale, current, total, from1, from2, new, work)
    send1[...] = new[pl.ds(odd, 15)]
    send2[...] = new[pl.ds(1 - odd, 15)]


def update(where, keep, scale, current, total, from1, from2, last):
    shapes = [PARTS[1]] if last else [PARTS[1], PARTS[0], PARTS[2]]
    return pl.pallas_call(
        add_neighbours if last else update_kernel,
        out_shape=[jax.ShapeDtypeStruct(s, F32) for s in shapes],
        in_specs=[SMEM] * 3 + [VMEM] * 4,
        out_specs=[VMEM] * len(shapes),
        scratch_shapes=[pltpu.VMEM(PARTS[1], F32)],
        compiler_params=pltpu.CompilerParams(vmem_limit_bytes=4 << 20),
        cost_estimate=pl.CostEstimate(flops=1_000_000, bytes_accessed=2_000_000, transcendentals=0),
        name="update",
    )(where, keep, scale, current, total, from1, from2)


def exchange(x, odd, tiles):
    pairs = []
    for t in range(odd, tiles, 2):
        pairs += [(t, (t + 1) % tiles), ((t + 1) % tiles, t)]
    return lax.ppermute(x, "tile", pairs)


def swap(x):
    return lax.ppermute(x, "view", [(0, 1), (1, 0)])


def per_device(estimate, view_data, psf_taps, coverage):
    tiles = lax.axis_size("tile")
    core = lax.axis_index("view")
    tile = lax.axis_index("tile")
    where = jnp.stack([core, tile, tile % 2]).astype(jnp.int32)
    current, send1, send2 = begin(where, estimate)
    other_current = swap(current)
    psf_taps, coverage, send1, send2 = lax.optimization_barrier((psf_taps, coverage, send1, send2))

    norm_taps = psf_taps / jnp.sum(psf_taps, axis=-1, keepdims=True)
    own = jnp.concatenate([norm_taps.reshape(-1), coverage.astype(F32).reshape(-1)])
    other, view_data = lax.optimization_barrier((swap(own), view_data))
    count = norm_taps.size
    taps = jnp.concatenate([own[:count], other[:count]])
    cover = jnp.concatenate([own[count:], other[count:]])
    ring = [(i, (i + 1) % tiles) for i in range(tiles)]
    before = lax.ppermute(cover, "tile", ring)
    after = lax.ppermute(cover, "tile", [(j, i) for i, j in ring])
    seen = jnp.sum(cover.reshape(VIEWS, W), axis=0)
    keep = 1.0 - jnp.minimum(seen, 1.0)
    scale = 1.0 / jnp.maximum(seen, 1.0)
    mine, theirs = rows(where, view_data)
    theirs = swap(theirs)
    xf, yf, yt, zf, zt = make_matrices(where, taps)
    xt = cover_matrix(where, taps, jnp.concatenate([before, cover, after]))

    for iteration in range(ITERS):
        last = iteration == ITERS - 1
        if iteration == 0:
            send1, send2 = exchange(send1, 1, tiles), exchange(send2, 0, tiles)
            others = blur(swap(send1), other_current, swap(send2), xf, zf)
            blurs = blur(send1, current, send2, xf, zf) + blur(send1, current, send2, xf, zf, PART)
            near, far = current[:, :PART], current[:, PART:]
        else:
            near1, near2 = exchange(near1, 1, tiles), exchange(near2, 0, tiles)
            far1, far2 = exchange(far1, 1, tiles), exchange(far2, 0, tiles)
            blurs = blur(near1, near, near2, xf, zf)
            others = blur(swap(near1), swap(near), swap(near2), xf, zf)
            far, others = lax.optimization_barrier((far, others))
            blurs = blurs + blur(far1, far, far2, xf, zf)
        near1, near_total, near2, far1, far_total, far2 = correct(blurs + others, mine, theirs, xt, yf, yt, zt)
        near1, near2 = exchange(near1, 1, tiles), exchange(near2, 0, tiles)
        far1, far2 = exchange(far1, 1, tiles), exchange(far2, 0, tiles)
        near, *sends = update(where, keep, scale, near, near_total, near1, near2, last)
        if not last:
            near1, near2 = sends
        far1, far2, near = lax.optimization_barrier((far1, far2, near))
        far, *sends = update(where, keep, scale, far, far_total, far1, far2, last)
        if not last:
            far1, far2 = sends

    zero = core == 0
    other_near, other_far = swap(near), swap(far)
    return jnp.concatenate(
        [
            jnp.where(zero, far, other_far),
            jnp.where(zero, near, other_near),
            jnp.where(zero, other_near, near),
            jnp.where(zero, other_far, far),
        ],
        1,
    )


def solution(mesh):
    return jax.shard_map(
        per_device,
        mesh=mesh,
        in_specs=(
            P("tile", None, None),
            P("view", "tile", None, None),
            P("view", None, None),
            P("view", "tile"),
        ),
        out_specs=P("tile", None, None),
        check_vma=False,
    )
```

```python
import functools

import jax
import jax.numpy as jnp
from jax import lax
from jax.experimental import pallas as pl
from jax.experimental.pallas import tpu as pltpu
from jax.sharding import PartitionSpec as P

ITERS = 4
TAPS = 31
REACH = 15
VIEWS = 6
W = 16
HALF = 64
EXT = 96
MID = 80
SLOTS = 48
NZ = 128
PART = 32
OWN_STEP = 65
PART_STEP = 33
F32 = jnp.float32
BF16 = jnp.bfloat16
VMEM = pl.BlockSpec(memory_space=pltpu.VMEM)
SMEM = pl.BlockSpec(memory_space=pltpu.SMEM)


def split(x):
    high = x.astype(BF16)
    return high, (x - high.astype(F32)).astype(BF16)


def dot(a, b):
    return jnp.dot(a, b, preferred_element_type=F32)


def iota(shape, dim):
    return lax.broadcasted_iota(jnp.int32, shape, dim)


def plane_of(slot, odd):
    middle = slot - REACH
    swapped = jnp.where(slot < REACH, slot + W, jnp.where(slot < REACH + W, middle, slot - 46))
    return jnp.where(odd == 0, middle, swapped)


def row_of(j, core):
    first = jnp.where(j < 32, j + 32, jnp.where(j < 64, j - 32, j))
    second = jnp.where(j < 64, j + 64, j - 32)
    return jnp.where(core == 0, first, second)


def mid_row_of(j, core):
    return jnp.where((core == 1) & (j >= 64), j - 16, row_of(j, core))


def put(ref, lead, rows, value):
    high, low = split(value)
    ref[lead + (pl.ds(0, rows),)] = high
    ref[lead + (pl.ds(rows, rows),)] = low


def select(taps, view, axis, index):
    total = jnp.zeros(index.shape, F32)
    for k in range(TAPS):
        total = jnp.where(index == k, taps[(view * 3 + axis) * TAPS + k], total)
    return total


def in_grid(slot, plane, tile):
    at = plane + W * tile
    return (slot < 46) & (at >= 0) & (at < 1024)


def matrices_kernel(where, taps, xf, yf, yt, zf, zt):
    core, tile, odd = where[0], where[1], where[2]

    shape = (VIEWS * W, 2 * SLOTS)
    slot = iota(shape, 1)
    slot = jnp.where(slot < SLOTS, slot, slot - SLOTS)
    plane = plane_of(slot, odd)
    row = iota(shape, 0)
    index = jnp.where(in_grid(slot, plane, tile), plane - row % W + REACH, -1)
    total = jnp.zeros(shape, F32)
    for view in range(VIEWS):
        total = jnp.where(row // W == view, select(taps, view, 0, index), total)
    put(xf, (), VIEWS * W, total)

    def per_view(view, _):
        shape = (MID, 2 * EXT)
        j = iota(shape, 1)
        j = jnp.where(j < EXT, j, j - EXT)
        index = row_of(j, core) - mid_row_of(iota(shape, 0), core) + REACH
        put(yf, (view,), MID, select(taps, view, 1, index))
        shape = (HALF, 2 * MID)
        j = iota(shape, 1)
        j = jnp.where(j < MID, j, j - MID)
        index = row_of(iota(shape, 0), core) - mid_row_of(j, core) + REACH
        put(yt, (view,), HALF, select(taps, view, 1, index))
        difference = iota((NZ, NZ), 0) - iota((NZ, NZ), 1)
        for ref, sign in ((zf, 1), (zt, -1)):
            high, low = split(select(taps, view, 2, sign * difference + REACH))
            for start in (0, NZ):
                ref[view, pl.ds(start, NZ), pl.ds(0, NZ)] = high
                ref[view, pl.ds(start, NZ), pl.ds(NZ, NZ)] = low
        return 0

    lax.fori_loop(0, VIEWS, per_view, 0)


def make_matrices(where, taps):
    shapes = [
        (2 * VIEWS * W, 2 * SLOTS),
        (VIEWS, 2 * MID, 2 * EXT),
        (VIEWS, 2 * HALF, 2 * MID),
        (VIEWS, 2 * NZ, 2 * NZ),
        (VIEWS, 2 * NZ, 2 * NZ),
    ]
    return pl.pallas_call(
        matrices_kernel,
        out_shape=[jax.ShapeDtypeStruct(s, BF16) for s in shapes],
        in_specs=[SMEM, SMEM],
        out_specs=[VMEM] * 5,
        compiler_params=pltpu.CompilerParams(vmem_limit_bytes=6 << 20),
        cost_estimate=pl.CostEstimate(flops=1_000, bytes_accessed=1_000, transcendentals=0),
        name="matrices",
    )(where, taps)


def cover_kernel(where, taps, cover, xt):
    core, tile, odd = where[0], where[1], where[2]
    shape = (SLOTS, 2 * VIEWS * W)
    slot = iota(shape, 0)
    plane = plane_of(slot, odd)
    column = iota(shape, 1)
    column = jnp.where(column < VIEWS * W, column, column - VIEWS * W)
    index = jnp.where(in_grid(slot, plane, tile), plane - column % W + REACH, -1)
    total = jnp.zeros(shape, F32)
    for view in range(VIEWS):
        covered = jnp.zeros((SLOTS, 2 * VIEWS * W), F32)
        for p in range(3 * W):
            covered = jnp.where(plane == p - W, cover[(p // W) * VIEWS * W + view * W + p % W], covered)
        total = jnp.where(column // W == view, select(taps, view, 0, index) * covered, total)
    put(xt, (), SLOTS, total)


def cover_matrix(where, taps, cover):
    return pl.pallas_call(
        cover_kernel,
        out_shape=jax.ShapeDtypeStruct((2 * SLOTS, 2 * VIEWS * W), BF16),
        in_specs=[SMEM, SMEM, SMEM],
        out_specs=VMEM,
        compiler_params=pltpu.CompilerParams(vmem_limit_bytes=2 << 20),
        cost_estimate=pl.CostEstimate(flops=1_000, bytes_accessed=1_000, transcendentals=0),
        name="cover_matrix",
    )(where, taps, cover)


def both(result):
    half = result.shape[0] // 2
    return result[:half] + result[half:]


def pair(result):
    return result[:, :NZ] + result[:, NZ:]


def beside(blocks):
    return jnp.concatenate(blocks, 1)


def along_x(source, target, matrix, rows, taken, given, source_step, target_step):
    group = 16

    def body(step, _):
        parts = [split(source[pl.ds(step * group + i, taken, stride=source_step)]) for i in range(group)]
        operand = jnp.concatenate([beside([p[0] for p in parts]), beside([p[1] for p in parts])], 0)
        result = both(dot(matrix[...], operand))
        for i in range(group):
            target[pl.ds(step * group + i, given, stride=target_step)] = result[:, i * NZ : (i + 1) * NZ]
        return 0

    lax.fori_loop(0, rows // group, body, 0)


def blur_kernel(at, first, own, second, xf, zf, out_high, out_low, ext, mid):
    slot = 0
    for source in (first, own, second):
        for i in range(source.shape[0]):
            ext[pl.ds(slot * PART_STEP, PART)] = source[i, pl.ds(at, PART)]
            slot += 1
    while slot < SLOTS:
        ext[pl.ds(slot * PART_STEP, PART)] = jnp.zeros((PART, NZ), F32)
        slot += 1
    along_x(ext, mid, xf, PART, SLOTS, VIEWS * W, PART_STEP, PART_STEP)

    def along_z(view, _):
        start = pl.multiple_of(view * (W * PART_STEP), 16)
        block = jnp.concatenate([mid[pl.ds(start + i * PART_STEP, PART)] for i in range(W)], 0)
        high, low = split(pair(dot(beside(split(block)), zf[view])))
        for i in range(W):
            out_high[view * W + i] = high[i * PART : (i + 1) * PART]
            out_low[view * W + i] = low[i * PART : (i + 1) * PART]
        return 0

    lax.fori_loop(0, VIEWS, along_z, 0, unroll=3)


def blur(first, own, second, xf, zf, at=0):
    return pl.pallas_call(
        functools.partial(blur_kernel, at),
        out_shape=[jax.ShapeDtypeStruct((VIEWS * W, PART, NZ), BF16)] * 2,
        in_specs=[VMEM] * 5,
        out_specs=[VMEM] * 2,
        scratch_shapes=[pltpu.VMEM(((SLOTS + 8) * PART_STEP, NZ), F32), pltpu.VMEM(((VIEWS * W + 8) * PART_STEP, NZ), F32)],
        compiler_params=pltpu.CompilerParams(vmem_limit_bytes=10 << 20),
        cost_estimate=pl.CostEstimate(flops=10_000_000_000, bytes_accessed=3_000_000, transcendentals=0),
        name="blur",
    )(first, own, second, xf, zf)


def correct_kernel(
    near_high, near_low, far_high, far_low, other_high, other_low, mine, theirs, xt, yf, yt, zt,
    near1, near_own, near2, far1, far_own, far2, back, wide,
):
    blurs = ((near_high, far_high, other_high), (near_low, far_low, other_low))

    def inner(data, base, unroll):
        def body(step, _):
            view = base + step
            operand = jnp.concatenate(
                [beside([ref[view * W + i] for i in range(W)]) for refs in blurs for ref in refs], 0
            )
            blurred = both(dot(yf[view], operand))
            measured = beside([data[step, i] for i in range(W)])
            result = both(dot(yt[view], jnp.concatenate(split(measured / blurred), 0)))
            block = jnp.concatenate([result[:, i * NZ : (i + 1) * NZ] for i in range(W)], 0)
            block = pair(dot(beside(split(block)), zt[view]))
            start = pl.multiple_of(view * (W * OWN_STEP), 16)
            for i in range(W):
                back[pl.ds(start + i * OWN_STEP, HALF)] = block[i * HALF : (i + 1) * HALF]
            return 0

        lax.fori_loop(0, VIEWS // 2, body, 0, unroll=unroll)

    inner(mine, 0, 3)
    inner(theirs, VIEWS // 2, 1)
    along_x(back, wide, xt, HALF, VIEWS * W, SLOTS, OWN_STEP, OWN_STEP)
    for at, outs in ((0, (near1, near_own, near2)), (PART, (far1, far_own, far2))):
        for slot, out in zip((0, 15, 31), outs):
            for i in range(out.shape[0]):
                out[i] = wide[pl.ds((slot + i) * OWN_STEP + at, PART)]


PARTS = [(15, PART, NZ), (16, PART, NZ), (15, PART, NZ)]


def correct(blurs, mine, theirs, xt, yf, yt, zt):
    return pl.pallas_call(
        correct_kernel,
        out_shape=[jax.ShapeDtypeStruct(s, F32) for s in PARTS * 2],
        in_specs=[VMEM] * 12,
        out_specs=[VMEM] * 6,
        scratch_shapes=[
            pltpu.VMEM(((VIEWS * W + 8) * OWN_STEP, NZ), F32),
            pltpu.VMEM(((SLOTS + 8) * OWN_STEP, NZ), F32),
        ],
        compiler_params=pltpu.CompilerParams(vmem_limit_bytes=26 << 20),
        cost_estimate=pl.CostEstimate(flops=4_000_000_000, bytes_accessed=16_000_000, transcendentals=0),
        name="correct",
    )(*blurs, mine, theirs, xt, yf, yt, zt)


def begin_kernel(where, estimate, current, send1, send2):
    core, odd = where[0], where[2]
    for start, at in ((32 + 32 * core, 0), (96 * core, PART)):
        rows = pl.ds(pl.multiple_of(start, 32), PART)
        for i in range(W):
            current[i, pl.ds(at, PART)] = estimate[i, rows]
    send1[...] = current[pl.ds(odd, 15)]
    send2[...] = current[pl.ds(1 - odd, 15)]


def begin(where, estimate):
    shapes = [(16, HALF, NZ), (15, HALF, NZ), (15, HALF, NZ)]
    return pl.pallas_call(
        begin_kernel,
        out_shape=[jax.ShapeDtypeStruct(s, F32) for s in shapes],
        in_specs=[SMEM, VMEM],
        out_specs=[VMEM] * 3,
        compiler_params=pltpu.CompilerParams(vmem_limit_bytes=6 << 20),
        cost_estimate=pl.CostEstimate(flops=1_000, bytes_accessed=1_000, transcendentals=0),
        name="begin",
    )(where, estimate)


def rows_kernel(where, data, mine, send):
    core = where[0]
    for ref, who in ((mine, core), (send, 1 - core)):
        for start, at, count in ((32 + 32 * who, 0, 32), (96 * who, 32, 32), (64 - 16 * who, 64, 16)):
            source = pl.ds(pl.multiple_of(start, 16), count)
            for view in range(VIEWS // 2):
                for i in range(W):
                    ref[view, i, pl.ds(at, count)] = data[view, i, source]


def rows(where, data):
    return pl.pallas_call(
        rows_kernel,
        out_shape=[jax.ShapeDtypeStruct((VIEWS // 2, W, MID, NZ), F32)] * 2,
        in_specs=[SMEM, VMEM],
        out_specs=[VMEM] * 2,
        compiler_params=pltpu.CompilerParams(vmem_limit_bytes=10 << 20),
        cost_estimate=pl.CostEstimate(flops=1_000, bytes_accessed=1_000, transcendentals=0),
        name="rows",
    )(where, data)


def add_neighbours(where, keep, scale, current, total, from1, from2, new, work):
    odd = where[2]
    work[...] = total[...]
    work[pl.ds(odd, 15)] += from1[...]
    work[pl.ds(1 - odd, 15)] += from2[...]
    for i in range(W):
        new[i] = current[i] * (work[i] + keep[i]) * scale[i]


def update_kernel(where, keep, scale, current, total, from1, from2, new, send1, send2, work):
    odd = where[2]
    add_neighbours(where, keep, scale, current, total, from1, from2, new, work)
    send1[...] = new[pl.ds(odd, 15)]
    send2[...] = new[pl.ds(1 - odd, 15)]


def update(where, keep, scale, current, total, from1, from2, last):
    shapes = [PARTS[1]] if last else [PARTS[1], PARTS[0], PARTS[2]]
    return pl.pallas_call(
        add_neighbours if last else update_kernel,
        out_shape=[jax.ShapeDtypeStruct(s, F32) for s in shapes],
        in_specs=[SMEM] * 3 + [VMEM] * 4,
        out_specs=[VMEM] * len(shapes),
        scratch_shapes=[pltpu.VMEM(PARTS[1], F32)],
        compiler_params=pltpu.CompilerParams(vmem_limit_bytes=4 << 20),
        cost_estimate=pl.CostEstimate(flops=1_000_000, bytes_accessed=2_000_000, transcendentals=0),
        name="update",
    )(where, keep, scale, current, total, from1, from2)


def exchange(x, odd, tiles):
    pairs = []
    for t in range(odd, tiles, 2):
        pairs += [(t, (t + 1) % tiles), ((t + 1) % tiles, t)]
    return lax.ppermute(x, "tile", pairs)


def swap(x):
    return lax.ppermute(x, "view", [(0, 1), (1, 0)])


def per_device(estimate, view_data, psf_taps, coverage):
    tiles = lax.axis_size("tile")
    core = lax.axis_index("view")
    tile = lax.axis_index("tile")
    where = jnp.stack([core, tile, tile % 2]).astype(jnp.int32)
    current, send1, send2 = begin(where, estimate)
    other_current = swap(current)
    psf_taps, coverage, send1, send2 = lax.optimization_barrier((psf_taps, coverage, send1, send2))

    norm_taps = psf_taps / jnp.sum(psf_taps, axis=-1, keepdims=True)
    own = jnp.concatenate([norm_taps.reshape(-1), coverage.astype(F32).reshape(-1)])
    other, view_data = lax.optimization_barrier((swap(own), view_data))
    count = norm_taps.size
    taps = jnp.concatenate([own[:count], other[:count]])
    cover = jnp.concatenate([own[count:], other[count:]])
    ring = [(i, (i + 1) % tiles) for i in range(tiles)]
    before = lax.ppermute(cover, "tile", ring)
    after = lax.ppermute(cover, "tile", [(j, i) for i, j in ring])
    seen = jnp.sum(cover.reshape(VIEWS, W), axis=0)
    keep = 1.0 - jnp.minimum(seen, 1.0)
    scale = 1.0 / jnp.maximum(seen, 1.0)
    mine, theirs = rows(where, view_data)
    theirs = swap(theirs)
    xf, yf, yt, zf, zt = make_matrices(where, taps)
    xt = cover_matrix(where, taps, jnp.concatenate([before, cover, after]))

    for iteration in range(ITERS):
        last = iteration == ITERS - 1
        if iteration == 0:
            send1, send2 = exchange(send1, 1, tiles), exchange(send2, 0, tiles)
            others = blur(swap(send1), other_current, swap(send2), xf, zf)
            blurs = blur(send1, current, send2, xf, zf) + blur(send1, current, send2, xf, zf, PART)
            near, far = current[:, :PART], current[:, PART:]
        else:
            near1, near2 = exchange(near1, 1, tiles), exchange(near2, 0, tiles)
            far1, far2 = exchange(far1, 1, tiles), exchange(far2, 0, tiles)
            blurs = blur(near1, near, near2, xf, zf)
            others = blur(swap(near1), swap(near), swap(near2), xf, zf)
            far, others = lax.optimization_barrier((far, others))
            blurs = blurs + blur(far1, far, far2, xf, zf)
        near1, near_total, near2, far1, far_total, far2 = correct(blurs + others, mine, theirs, xt, yf, yt, zt)
        near1, near2 = exchange(near1, 1, tiles), exchange(near2, 0, tiles)
        far1, far2 = exchange(far1, 1, tiles), exchange(far2, 0, tiles)
        near, *sends = update(where, keep, scale, near, near_total, near1, near2, last)
        if not last:
            near1, near2 = sends
        far1, far2, near = lax.optimization_barrier((far1, far2, near))
        far, *sends = update(where, keep, scale, far, far_total, far1, far2, last)
        if not last:
            far1, far2 = sends

    zero = core == 0
    other_near, other_far = swap(near), swap(far)
    return jnp.concatenate(
        [
            jnp.where(zero, far, other_far),
            jnp.where(zero, near, other_near),
            jnp.where(zero, other_near, near),
            jnp.where(zero, other_far, far),
        ],
        1,
    )


def solution(mesh):
    return jax.shard_map(
        per_device,
        mesh=mesh,
        in_specs=(
            P("tile", None, None),
            P("view", "tile", None, None),
            P("view", None, None),
            P("view", "tile"),
        ),
        out_specs=P("tile", None, None),
        check_vma=False,
    )
```

```python
import functools

import jax
import jax.numpy as jnp
from jax import lax
from jax.experimental import pallas as pl
from jax.experimental.pallas import tpu as pltpu
from jax.sharding import PartitionSpec as P

ITERS = 4
TAPS = 31
REACH = 15
VIEWS = 6
W = 16
HALF = 64
EXT = 96
MID = 80
SLOTS = 48
NZ = 128
PART = 32
OWN_STEP = 65
PART_STEP = 33
F32 = jnp.float32
BF16 = jnp.bfloat16
VMEM = pl.BlockSpec(memory_space=pltpu.VMEM)
SMEM = pl.BlockSpec(memory_space=pltpu.SMEM)


def split(x):
    high = x.astype(BF16)
    return high, (x - high.astype(F32)).astype(BF16)


def dot(a, b):
    return jnp.dot(a, b, preferred_element_type=F32)


def iota(shape, dim):
    return lax.broadcasted_iota(jnp.int32, shape, dim)


def plane_of(slot, odd):
    middle = slot - REACH
    swapped = jnp.where(slot < REACH, slot + W, jnp.where(slot < REACH + W, middle, slot - 46))
    return jnp.where(odd == 0, middle, swapped)


def row_of(j, core):
    first = jnp.where(j < 32, j + 32, jnp.where(j < 64, j - 32, j))
    second = jnp.where(j < 64, j + 64, j - 32)
    return jnp.where(core == 0, first, second)


def mid_row_of(j, core):
    return jnp.where((core == 1) & (j >= 64), j - 16, row_of(j, core))


def put(ref, lead, rows, value):
    high, low = split(value)
    ref[lead + (pl.ds(0, rows),)] = high
    ref[lead + (pl.ds(rows, rows),)] = low


def three(value, column, width):
    high = value.astype(BF16).astype(F32)
    return jnp.where((column >= width) & (column < 2 * width), value - high, high).astype(BF16)


def thirds(column, width):
    return column - jnp.where(column >= 2 * width, 2 * width, jnp.where(column >= width, width, 0))


def select(taps, view, axis, index):
    total = jnp.zeros(index.shape, F32)
    for k in range(TAPS):
        total = jnp.where(index == k, taps[(view * 3 + axis) * TAPS + k], total)
    return total


def in_grid(slot, plane, tile):
    at = plane + W * tile
    return (slot < 46) & (at >= 0) & (at < 1024)


def matrices_kernel(where, taps, xf, yf, yt, zf, zt):
    core, tile, odd = where[0], where[1], where[2]

    shape = (VIEWS * W, 3 * SLOTS)
    column = iota(shape, 1)
    slot = thirds(column, SLOTS)
    plane = plane_of(slot, odd)
    row = iota(shape, 0)
    index = jnp.where(in_grid(slot, plane, tile), plane - row % W + REACH, -1)
    total = jnp.zeros(shape, F32)
    for view in range(VIEWS):
        total = jnp.where(row // W == view, select(taps, view, 0, index), total)
    xf[...] = three(total, column, SLOTS)

    def per_view(view, _):
        shape = (MID, 2 * EXT)
        j = iota(shape, 1)
        j = jnp.where(j < EXT, j, j - EXT)
        index = row_of(j, core) - mid_row_of(iota(shape, 0), core) + REACH
        put(yf, (view,), MID, select(taps, view, 1, index))
        shape = (HALF, 3 * MID)
        column = iota(shape, 1)
        j = thirds(column, MID)
        index = row_of(iota(shape, 0), core) - mid_row_of(j, core) + REACH
        yt[view] = three(select(taps, view, 1, index), column, MID)
        difference = iota((NZ, NZ), 0) - iota((NZ, NZ), 1)
        for ref, sign in ((zf, 1), (zt, -1)):
            high, low = split(select(taps, view, 2, sign * difference + REACH))
            for start in (0, NZ):
                ref[view, pl.ds(start, NZ), pl.ds(0, NZ)] = high
                ref[view, pl.ds(start, NZ), pl.ds(NZ, NZ)] = low
        return 0

    lax.fori_loop(0, VIEWS, per_view, 0)


def make_matrices(where, taps):
    shapes = [
        (VIEWS * W, 3 * SLOTS),
        (VIEWS, 2 * MID, 2 * EXT),
        (VIEWS, HALF, 3 * MID),
        (VIEWS, 2 * NZ, 2 * NZ),
        (VIEWS, 2 * NZ, 2 * NZ),
    ]
    return pl.pallas_call(
        matrices_kernel,
        out_shape=[jax.ShapeDtypeStruct(s, BF16) for s in shapes],
        in_specs=[SMEM, SMEM],
        out_specs=[VMEM] * 5,
        compiler_params=pltpu.CompilerParams(vmem_limit_bytes=6 << 20),
        cost_estimate=pl.CostEstimate(flops=1_000, bytes_accessed=1_000, transcendentals=0),
        name="matrices",
    )(where, taps)


def cover_kernel(where, taps, cover, xt):
    core, tile, odd = where[0], where[1], where[2]
    shape = (SLOTS, 2 * VIEWS * W)
    slot = iota(shape, 0)
    plane = plane_of(slot, odd)
    column = iota(shape, 1)
    column = jnp.where(column < VIEWS * W, column, column - VIEWS * W)
    index = jnp.where(in_grid(slot, plane, tile), plane - column % W + REACH, -1)
    total = jnp.zeros(shape, F32)
    for view in range(VIEWS):
        covered = jnp.zeros((SLOTS, 2 * VIEWS * W), F32)
        for p in range(3 * W):
            covered = jnp.where(plane == p - W, cover[(p // W) * VIEWS * W + view * W + p % W], covered)
        total = jnp.where(column // W == view, select(taps, view, 0, index) * covered, total)
    put(xt, (), SLOTS, total)


def cover_matrix(where, taps, cover):
    return pl.pallas_call(
        cover_kernel,
        out_shape=jax.ShapeDtypeStruct((2 * SLOTS, 2 * VIEWS * W), BF16),
        in_specs=[SMEM, SMEM, SMEM],
        out_specs=VMEM,
        compiler_params=pltpu.CompilerParams(vmem_limit_bytes=2 << 20),
        cost_estimate=pl.CostEstimate(flops=1_000, bytes_accessed=1_000, transcendentals=0),
        name="cover_matrix",
    )(where, taps, cover)


def both(result):
    half = result.shape[0] // 2
    return result[:half] + result[half:]


def pair(result):
    return result[:, :NZ] + result[:, NZ:]


def beside(blocks):
    return jnp.concatenate(blocks, 1)


def along_x(source, target, matrix, rows, taken, given, source_step, target_step, products):
    group = 16

    def body(step, _):
        parts = [split(source[pl.ds(step * group + i, taken, stride=source_step)]) for i in range(group)]
        high, low = beside([p[0] for p in parts]), beside([p[1] for p in parts])
        if products == 3:
            result = dot(matrix[...], jnp.concatenate([high, high, low], 0))
        else:
            result = both(dot(matrix[...], jnp.concatenate([high, low], 0)))
        for i in range(group):
            target[pl.ds(step * group + i, given, stride=target_step)] = result[:, i * NZ : (i + 1) * NZ]
        return 0

    lax.fori_loop(0, rows // group, body, 0)


def blur_kernel(at, first, own, second, xf, zf, out_high, out_low, ext, mid):
    slot = 0
    for source in (first, own, second):
        for i in range(source.shape[0]):
            ext[pl.ds(slot * PART_STEP, PART)] = source[i, pl.ds(at, PART)]
            slot += 1
    while slot < SLOTS:
        ext[pl.ds(slot * PART_STEP, PART)] = jnp.zeros((PART, NZ), F32)
        slot += 1
    along_x(ext, mid, xf, PART, SLOTS, VIEWS * W, PART_STEP, PART_STEP, 3)

    def along_z(view, _):
        start = pl.multiple_of(view * (W * PART_STEP), 16)
        block = jnp.concatenate([mid[pl.ds(start + i * PART_STEP, PART)] for i in range(W)], 0)
        high, low = split(pair(dot(beside(split(block)), zf[view])))
        for i in range(W):
            out_high[view * W + i] = high[i * PART : (i + 1) * PART]
            out_low[view * W + i] = low[i * PART : (i + 1) * PART]
        return 0

    lax.fori_loop(0, VIEWS, along_z, 0, unroll=3)


def blur(first, own, second, xf, zf, at=0):
    return pl.pallas_call(
        functools.partial(blur_kernel, at),
        out_shape=[jax.ShapeDtypeStruct((VIEWS * W, PART, NZ), BF16)] * 2,
        in_specs=[VMEM] * 5,
        out_specs=[VMEM] * 2,
        scratch_shapes=[pltpu.VMEM(((SLOTS + 8) * PART_STEP, NZ), F32), pltpu.VMEM(((VIEWS * W + 8) * PART_STEP, NZ), F32)],
        compiler_params=pltpu.CompilerParams(vmem_limit_bytes=10 << 20),
        cost_estimate=pl.CostEstimate(flops=10_000_000_000, bytes_accessed=3_000_000, transcendentals=0),
        name="blur",
    )(first, own, second, xf, zf)


def correct_kernel(
    near_high, near_low, far_high, far_low, other_high, other_low, mine, theirs, xt, yf, yt, zt,
    near1, near_own, near2, far1, far_own, far2, back, wide,
):
    blurs = ((near_high, far_high, other_high), (near_low, far_low, other_low))

    def inner(data, base, unroll):
        def body(step, _):
            view = base + step
            operand = jnp.concatenate(
                [beside([ref[view * W + i] for i in range(W)]) for refs in blurs for ref in refs], 0
            )
            blurred = both(dot(yf[view], operand))
            measured = beside([data[step, i] for i in range(W)])
            high, low = split(measured / blurred)
            result = dot(yt[view], jnp.concatenate([high, high, low], 0))
            block = jnp.concatenate([result[:, i * NZ : (i + 1) * NZ] for i in range(W)], 0)
            block = pair(dot(beside(split(block)), zt[view]))
            start = pl.multiple_of(view * (W * OWN_STEP), 16)
            for i in range(W):
                back[pl.ds(start + i * OWN_STEP, HALF)] = block[i * HALF : (i + 1) * HALF]
            return 0

        lax.fori_loop(0, VIEWS // 2, body, 0, unroll=unroll)

    inner(mine, 0, 3)
    inner(theirs, VIEWS // 2, 1)
    along_x(back, wide, xt, HALF, VIEWS * W, SLOTS, OWN_STEP, OWN_STEP, 4)
    for at, outs in ((0, (near1, near_own, near2)), (PART, (far1, far_own, far2))):
        for slot, out in zip((0, 15, 31), outs):
            for i in range(out.shape[0]):
                out[i] = wide[pl.ds((slot + i) * OWN_STEP + at, PART)]


PARTS = [(15, PART, NZ), (16, PART, NZ), (15, PART, NZ)]


def correct(blurs, mine, theirs, xt, yf, yt, zt):
    return pl.pallas_call(
        correct_kernel,
        out_shape=[jax.ShapeDtypeStruct(s, F32) for s in PARTS * 2],
        in_specs=[VMEM] * 12,
        out_specs=[VMEM] * 6,
        scratch_shapes=[
            pltpu.VMEM(((VIEWS * W + 8) * OWN_STEP, NZ), F32),
            pltpu.VMEM(((SLOTS + 8) * OWN_STEP, NZ), F32),
        ],
        compiler_params=pltpu.CompilerParams(vmem_limit_bytes=26 << 20),
        cost_estimate=pl.CostEstimate(flops=4_000_000_000, bytes_accessed=16_000_000, transcendentals=0),
        name="correct",
    )(*blurs, mine, theirs, xt, yf, yt, zt)


def begin_kernel(where, estimate, current, send1, send2):
    core, odd = where[0], where[2]
    for start, at in ((32 + 32 * core, 0), (96 * core, PART)):
        rows = pl.ds(pl.multiple_of(start, 32), PART)
        for i in range(W):
            current[i, pl.ds(at, PART)] = estimate[i, rows]
    send1[...] = current[pl.ds(odd, 15)]
    send2[...] = current[pl.ds(1 - odd, 15)]


def begin(where, estimate):
    shapes = [(16, HALF, NZ), (15, HALF, NZ), (15, HALF, NZ)]
    return pl.pallas_call(
        begin_kernel,
        out_shape=[jax.ShapeDtypeStruct(s, F32) for s in shapes],
        in_specs=[SMEM, VMEM],
        out_specs=[VMEM] * 3,
        compiler_params=pltpu.CompilerParams(vmem_limit_bytes=6 << 20),
        cost_estimate=pl.CostEstimate(flops=1_000, bytes_accessed=1_000, transcendentals=0),
        name="begin",
    )(where, estimate)


def rows_kernel(where, data, mine, send):
    core = where[0]
    for ref, who in ((mine, core), (send, 1 - core)):
        for start, at, count in ((32 + 32 * who, 0, 32), (96 * who, 32, 32), (64 - 16 * who, 64, 16)):
            source = pl.ds(pl.multiple_of(start, 16), count)
            for view in range(VIEWS // 2):
                for i in range(W):
                    ref[view, i, pl.ds(at, count)] = data[view, i, source]


def rows(where, data):
    return pl.pallas_call(
        rows_kernel,
        out_shape=[jax.ShapeDtypeStruct((VIEWS // 2, W, MID, NZ), F32)] * 2,
        in_specs=[SMEM, VMEM],
        out_specs=[VMEM] * 2,
        compiler_params=pltpu.CompilerParams(vmem_limit_bytes=10 << 20),
        cost_estimate=pl.CostEstimate(flops=1_000, bytes_accessed=1_000, transcendentals=0),
        name="rows",
    )(where, data)


def add_neighbours(where, keep, scale, current, total, from1, from2, new, work):
    odd = where[2]
    work[...] = total[...]
    work[pl.ds(odd, 15)] += from1[...]
    work[pl.ds(1 - odd, 15)] += from2[...]
    for i in range(W):
        new[i] = current[i] * (work[i] + keep[i]) * scale[i]


def update_kernel(where, keep, scale, current, total, from1, from2, new, send1, send2, work):
    odd = where[2]
    add_neighbours(where, keep, scale, current, total, from1, from2, new, work)
    send1[...] = new[pl.ds(odd, 15)]
    send2[...] = new[pl.ds(1 - odd, 15)]


def update(where, keep, scale, current, total, from1, from2, last):
    shapes = [PARTS[1]] if last else [PARTS[1], PARTS[0], PARTS[2]]
    return pl.pallas_call(
        add_neighbours if last else update_kernel,
        out_shape=[jax.ShapeDtypeStruct(s, F32) for s in shapes],
        in_specs=[SMEM] * 3 + [VMEM] * 4,
        out_specs=[VMEM] * len(shapes),
        scratch_shapes=[pltpu.VMEM(PARTS[1], F32)],
        compiler_params=pltpu.CompilerParams(vmem_limit_bytes=4 << 20),
        cost_estimate=pl.CostEstimate(flops=1_000_000, bytes_accessed=2_000_000, transcendentals=0),
        name="update",
    )(where, keep, scale, current, total, from1, from2)


def exchange(x, odd, tiles):
    pairs = []
    for t in range(odd, tiles, 2):
        pairs += [(t, (t + 1) % tiles), ((t + 1) % tiles, t)]
    return lax.ppermute(x, "tile", pairs)


def swap(x):
    return lax.ppermute(x, "view", [(0, 1), (1, 0)])


def per_device(estimate, view_data, psf_taps, coverage):
    tiles = lax.axis_size("tile")
    core = lax.axis_index("view")
    tile = lax.axis_index("tile")
    where = jnp.stack([core, tile, tile % 2]).astype(jnp.int32)
    current, send1, send2 = begin(where, estimate)
    other_current = swap(current)
    psf_taps, coverage, send1, send2 = lax.optimization_barrier((psf_taps, coverage, send1, send2))

    norm_taps = psf_taps / jnp.sum(psf_taps, axis=-1, keepdims=True)
    own = jnp.concatenate([norm_taps.reshape(-1), coverage.astype(F32).reshape(-1)])
    other, view_data = lax.optimization_barrier((swap(own), view_data))
    count = norm_taps.size
    taps = jnp.concatenate([own[:count], other[:count]])
    cover = jnp.concatenate([own[count:], other[count:]])
    ring = [(i, (i + 1) % tiles) for i in range(tiles)]
    before = lax.ppermute(cover, "tile", ring)
    after = lax.ppermute(cover, "tile", [(j, i) for i, j in ring])
    seen = jnp.sum(cover.reshape(VIEWS, W), axis=0)
    keep = 1.0 - jnp.minimum(seen, 1.0)
    scale = 1.0 / jnp.maximum(seen, 1.0)
    mine, theirs = rows(where, view_data)
    theirs = swap(theirs)
    xf, yf, yt, zf, zt = make_matrices(where, taps)
    xt = cover_matrix(where, taps, jnp.concatenate([before, cover, after]))

    for iteration in range(ITERS):
        last = iteration == ITERS - 1
        if iteration == 0:
            send1, send2 = exchange(send1, 1, tiles), exchange(send2, 0, tiles)
            others = blur(swap(send1), other_current, swap(send2), xf, zf)
            blurs = blur(send1, current, send2, xf, zf) + blur(send1, current, send2, xf, zf, PART)
            near, far = current[:, :PART], current[:, PART:]
        else:
            near1, near2 = exchange(near1, 1, tiles), exchange(near2, 0, tiles)
            far1, far2 = exchange(far1, 1, tiles), exchange(far2, 0, tiles)
            blurs = blur(near1, near, near2, xf, zf)
            others = blur(swap(near1), swap(near), swap(near2), xf, zf)
            far, others = lax.optimization_barrier((far, others))
            blurs = blurs + blur(far1, far, far2, xf, zf)
        near1, near_total, near2, far1, far_total, far2 = correct(blurs + others, mine, theirs, xt, yf, yt, zt)
        near1, near2 = exchange(near1, 1, tiles), exchange(near2, 0, tiles)
        far1, far2 = exchange(far1, 1, tiles), exchange(far2, 0, tiles)
        near, *sends = update(where, keep, scale, near, near_total, near1, near2, last)
        if not last:
            near1, near2 = sends
        far1, far2, near = lax.optimization_barrier((far1, far2, near))
        far, *sends = update(where, keep, scale, far, far_total, far1, far2, last)
        if not last:
            far1, far2 = sends

    zero = core == 0
    other_near, other_far = swap(near), swap(far)
    return jnp.concatenate(
        [
            jnp.where(zero, far, other_far),
            jnp.where(zero, near, other_near),
            jnp.where(zero, other_near, near),
            jnp.where(zero, other_far, far),
        ],
        1,
    )


def solution(mesh):
    return jax.shard_map(
        per_device,
        mesh=mesh,
        in_specs=(
            P("tile", None, None),
            P("view", "tile", None, None),
            P("view", None, None),
            P("view", "tile"),
        ),
        out_specs=P("tile", None, None),
        check_vma=False,
    )
```
